256 devices in a mesh: wide: 32 (over y, z), narrow: 8 (over x, core).
Axes of the slice: x: 4, y: 4, z: 8, core: 2. Of those that a mesh axis runs over, the one named last changes fastest.
Arguments:
- residual: bfloat16 [32, 8, 2048, 256], P('wide', 'narrow'), may hold values from -6 to 6
- scaling: float32 [32, 8, 2048], P('wide', 'narrow'), may hold values from 0.25 to 1
- local_inverse: bfloat16 [32, 8, 2048, 2048], P('wide', 'narrow'), may hold values from -0.125 to 0.125
- coarse_basis: bfloat16 [32, 8, 24, 2048], P('wide', 'narrow'), may hold values from -0.125 to 0.125
- primal_map: int32 [32, 8, 24], P('wide', 'narrow'), may hold values from 0 to 191
- slot_index: int32 [32, 8, 10, 256], P('wide', 'narrow'), may hold values from 0 to 2047, as said below
- slot_length: int32 [32, 8, 10], P('wide', 'narrow'), may hold values from 0 to 256, as said below
- coarse_sub: float32 [32, 192, 192], P('wide'), may hold values from -0.4375 to 0.4375
- coarse_pivot: float32 [32, 192, 192], P('wide'), as said below
Outputs:
- interface_sum: float32 [32, 8, 2048, 256], P('wide', 'narrow')
The draws below stay inside these ranges and needn't reach their ends.
Inputs may be any that keep to these rules, and one draw needn't show every extreme that they name: `slot_index`: within one slot of one subdomain the 256 entries are distinct. `slot_length`: paired slots have equal lengths: slot j of subdomain (w, n) and slot n of (w, j); slot 8 of (w, n) and slot 9 of (w - 1, n). A subdomain's own narrow slot n, the slot 8 of slab 0 and the slot 9 of slab 32 - 1 have length 0. `coarse_pivot`: Symmetric.
All inputs are finite; a program needn't handle non-finite values.
Results may differ from the reference program's by a relative error of at most 0.0039.
The reference program's roundings to bfloat16 on the way (of `weighted`, `combined`, `outgoing` and `incoming`) count: a program that leaves them out, or rounds other values in their place, can miss the bound.
Values may be sent and summed in bfloat16 or wider, within the bound.
A program may use at most 128 MiB of HBM per device.

```python
import math
import jax
import jax.numpy as jnp
from jax import lax

NI = 2048
R = 256
P_SIZE = 24
B = 256
NW = 32
NN = 8
G = 192


def draw_slot_length(key, part):
    first_key, second_key = jax.random.split(jax.random.fold_in(key, 11))
    paired = jax.random.randint(first_key, (NW, NN, NN), B // 4, B + 1)
    paired = paired.at[:, 0, 1].set(B)
    counter = jnp.arange(NN)
    upper_tri = counter[:, None] < counter[None, :]
    narrow = jnp.where(upper_tri[None], paired, jnp.swapaxes(paired, 1, 2))
    narrow = jnp.where((counter[:, None] == counter[None, :])[None], 0, narrow)
    links = jax.random.randint(second_key, (NW, NN), B // 4, B + 1)
    slabs = jnp.arange(NW)[:, None]
    upper = jnp.where(slabs < NW - 1, links, 0)
    lower = jnp.where(slabs > 0, jnp.roll(links, 1, axis=0), 0)
    return jnp.concatenate([narrow, lower[:, :, None], upper[:, :, None]], axis=2).astype(jnp.int32)


def draw_slot_index(key, part):
    scores = jax.random.randint(jax.random.fold_in(key, 23), (NW, NN, NN + 2, NI), 0, 1024)
    scores = scores * NI + jnp.arange(NI, dtype=jnp.int32)
    scores = scores.at[0, 0, 0, 0].set(-2)
    scores = scores.at[0, 0, 0, NI - 1].set(-1)
    order = jnp.argsort(scores, axis=-1)
    return order[..., :B].astype(jnp.int32)


def draw_coarse_pivot(key, part):
    first_key, second_key = jax.random.split(jax.random.fold_in(key, 37))
    offdiag = jax.random.uniform(first_key, (NW, G, G), jnp.float32, -1.0, 1.0) * (2.0 / G)
    offdiag = 0.5 * (offdiag + jnp.swapaxes(offdiag, 1, 2))
    diagonal = jax.random.uniform(second_key, (NW, G), jnp.float32, 0.5, 2.0)
    identity = jnp.eye(G, dtype=jnp.float32)
    return (offdiag * (1.0 - identity)[None] + diagonal[:, :, None] * identity[None]).astype(jnp.float32)


def with_ends(values, own_key, least, largest):
    longest = values.shape.index(max(values.shape))
    spots = []
    for shift in (0, 1):
        where = [jax.random.randint(jax.random.fold_in(own_key, axis), (), 0, length) for axis, length in enumerate(values.shape)]
        where[longest] = (where[longest] + shift) % values.shape[longest]
        spots.append(tuple(where))
    return values.at[spots[0]].set(least).at[spots[1]].set(largest)


def levels(key, dims, shards, low, high):
    loudness, own = 1.0, jax.random.fold_in(key, 6)
    for position, parts in shards:
        steps = jnp.exp(jax.random.uniform(jax.random.fold_in(own, position), (parts,), jnp.float32, low / len(shards), high / len(shards)))
        loudness = loudness * jnp.repeat(steps, dims[position] // parts).reshape([-1 if axis == position else 1 for axis in range(len(dims))])
    return loudness


def centred(own_key, extent, width, reach, shards=(), kind=jnp.bfloat16):
    gain = levels(own_key, extent, shards, -0.22, 0.18) if shards else 1.0
    entries = jax.random.normal(own_key, extent, jnp.float32) * width * gain
    return jnp.minimum(jnp.maximum(entries, -reach), reach).astype(kind)


def setup_inputs(seed: int = 0) -> dict:
    keys = jax.random.split(jax.random.key(seed), 10)
    residual = centred(keys[0], (NW, NN, NI, R), 1.0, 6.0, ((0, 32), (1, 8)))
    scaling = jnp.clip(jnp.exp(math.log(1.0) - 1.3862944 * jax.random.uniform(keys[1], (NW, NN, NI), jnp.float32) ** levels(keys[1], (NW, NN, NI), ((0, 32), (1, 8)), -0.2, 0.2)), 0.25, 1.0)
    local_inverse = centred(keys[2], (NW, NN, NI, NI), NI ** -0.5, 0.125, ((0, 32), (1, 8)))
    coarse_basis = centred(keys[3], (NW, NN, P_SIZE, NI), NI ** -0.5, 0.125, ((0, 32), (1, 8)))
    primal_map = with_ends(jax.random.randint(keys[4], (NW, NN, P_SIZE), 0, G), jax.random.fold_in(keys[4], 1), 0, G - 1).astype(jnp.int32)
    slot_index = draw_slot_index(jax.random.fold_in(keys[9], 71), 0)
    slot_length = draw_slot_length(jax.random.fold_in(keys[9], 71), 0)
    coarse_sub = centred(keys[7], (NW, G, G), G ** -0.5, 0.4375, ((0, 32),), jnp.float32)
    coarse_pivot = draw_coarse_pivot(jax.random.fold_in(keys[9], 71), 0)
    return {"residual": residual, "scaling": scaling, "local_inverse": local_inverse, "coarse_basis": coarse_basis, "primal_map": primal_map, "slot_index": slot_index, "slot_length": slot_length, "coarse_sub": coarse_sub, "coarse_pivot": coarse_pivot}


highest = lax.Precision.HIGHEST


def exact_dot(left, right):
    return jnp.dot(left, right, precision=highest, preferred_element_type=jnp.float32)


def solve_local(operands):
    return jnp.dot(operands[0], operands[1], preferred_element_type=jnp.float32)


def add_rows(base, where, values):
    return base.at[where.reshape(-1)].add(values.reshape(-1, values.shape[-1]))


def pick_rows(rows, where):
    return rows[where]


def reference(residual, scaling, local_inverse, coarse_basis, primal_map, slot_index, slot_length, coarse_sub, coarse_pivot):
    weighted = (scaling[..., None] * residual.astype(jnp.float32)).astype(jnp.bfloat16)
    flat_inverse = local_inverse.reshape(NW * NN, NI, NI)
    flat_rhs = weighted.reshape(NW * NN, NI, R)
    local_part = lax.map(solve_local, (flat_inverse, flat_rhs)).reshape(NW, NN, NI, R)
    basis_full = coarse_basis.astype(jnp.float32)
    primal = jnp.einsum("wnpi,wnir->wnpr", basis_full, weighted.astype(jnp.float32), precision=highest)
    one_hot = (primal_map[..., None] == jnp.arange(G, dtype=jnp.int32)).astype(jnp.float32)
    coarse_rhs = jnp.einsum("wnpg,wnpr->wgr", one_hot, primal, precision=highest)

    def forward(carry, inputs):
        value = inputs[1] - exact_dot(inputs[0], carry)
        return value, value

    final_y, chain_y = lax.scan(forward, jnp.zeros((G, R), jnp.float32), (coarse_sub, coarse_rhs))
    pivoted = jnp.einsum("wgh,whr->wgr", coarse_pivot, chain_y, precision=highest)

    def backward(carry, inputs):
        solved = inputs[1] - carry
        transfer = exact_dot(inputs[0].T, inputs[1]) - exact_dot(inputs[0].T, carry)
        return transfer, solved

    final_t, coarse_sol = lax.scan(backward, jnp.zeros((G, R), jnp.float32), (coarse_sub, pivoted), reverse=True)
    coarse_vals = jnp.einsum("wnpg,wgr->wnpr", one_hot, coarse_sol, precision=highest)
    spread = jnp.einsum("wnpi,wnpr->wnir", basis_full, coarse_vals, precision=highest)
    combined = (scaling[..., None] * (local_part + spread)).astype(jnp.bfloat16)
    live = jnp.arange(B, dtype=jnp.int32)[None, None, None, :] < slot_length[..., None]
    picked = jax.vmap(jax.vmap(pick_rows))(combined, slot_index)
    outgoing = jnp.where(live[..., None], picked, jnp.zeros((), jnp.bfloat16))
    narrow_in = jnp.swapaxes(outgoing[:, :, :NN], 1, 2)
    zero_slab = jnp.zeros_like(outgoing[:1, :, NN])
    below = jnp.concatenate([zero_slab, outgoing[:-1, :, NN + 1]], axis=0)
    above = jnp.concatenate([outgoing[1:, :, NN], zero_slab], axis=0)
    incoming = jnp.concatenate([narrow_in, below[:, :, None], above[:, :, None]], axis=2)
    return jax.vmap(jax.vmap(add_rows))(combined.astype(jnp.float32), slot_index, incoming.astype(jnp.float32))
```

```python
import jax
import jax.numpy as jnp
from jax import lax
from jax.experimental import pallas as pl
from jax.experimental.pallas import tpu as pltpu
from jax.sharding import PartitionSpec as P

MESH = pl.DeviceIdType.MESH
f32 = jnp.float32
bf16 = jnp.bfloat16
NZ = 8
NY = 4
NN = 8
NS = 10
NI = 2048
R = 256
PC = 24
G = 192
CH = R // NN
PIECE = G // NN
CARRY = CH + G
TILE = 256


def owner_z(n):
    return n // 2 + 4 * (n % 2)


def iota(shape, axis):
    return lax.broadcasted_iota(jnp.int32, shape, axis)


def split2(a):
    high = a.astype(bf16)
    return high, (a - high.astype(f32)).astype(bf16)


def split3(a):
    high = a.astype(bf16)
    rest = a - high.astype(f32)
    middle = rest.astype(bf16)
    return high, middle, (rest - middle.astype(f32)).astype(bf16)


def nn(a, b):
    return lax.dot_general(a, b, (((1,), (0,)), ((), ())), preferred_element_type=f32)


def nt(a, b):
    return lax.dot_general(a, b, (((1,), (1,)), ((), ())), preferred_element_type=f32)


def dot3(dot, a, b):
    a_high, a_low = split2(a)
    b_high, b_low = split2(b)
    return dot(a_high, b_high) + (dot(a_high, b_low) + dot(a_low, b_high))


def kernel(
    res_hbm, scal_ref, inv_hbm, basis_ref, pmap_ref, sidx_ref, slen_ref, sub_hbm, piv_hbm,
    out_hbm,
    res, inv, wgt, local, rows, ext, select, pick_out, pick_in, inc, result,
    idxm, tiles, maps, spread_map, vals, xfull, stack,
    prim_in, prim_v, sub, piv, chain, rhs, planes, high_carry, pivoted, xs, xplanes, carry,
    load_sem, inv_sem, out_sem,
    prim_send, prim_recv, sub_send, sub_recv, piv_send, piv_recv,
    map_send, map_recv, pick_send, pick_recv,
    y_send, y_recv, t_send, t_recv, b_send, b_recv,
    x_send, x_recv, gather_send, gather_recv, val_send, val_recv,
):
    w = lax.axis_index("wide")
    n = lax.axis_index("narrow")
    y = w // NZ
    z = w % NZ
    base = y * NZ
    above = lax.rem(w + 1, NY * NZ)
    below = lax.rem(w + NY * NZ - 1, NY * NZ)
    is_owner = z == owner_z(n)

    load = pltpu.make_async_copy(res_hbm.at[0, 0], res, load_sem)
    load.start()

    def inv_load(i):
        at = pl.ds(pl.multiple_of(i * TILE, TILE), TILE)
        return pltpu.make_async_copy(inv_hbm.at[0, 0, at], inv.at[at], inv_sem.at[i])

    @pl.loop(0, NI // TILE)
    def _(i):
        inv_load(i).start()

    barrier = pltpu.get_barrier_semaphore()

    def hello(device):
        pl.semaphore_signal(barrier, inc=1, device_id=device, device_id_type=MESH)

    for d in range(1, NN):
        hello((w, lax.rem(n + d, NN)))
    hello((above, n))
    hello((below, n))

    @pl.when(is_owner)
    def _():
        @pl.loop(1, NZ * NN)
        def _(d):
            at = lax.rem(z * NN + n + d, NZ * NN)
            hello((base + at // NN, at % NN))

        for d in range(1, NY):
            hello((lax.rem(y + d, NY) * NZ + z, n))

    @pl.when(jnp.logical_not(is_owner))
    def _():
        hello((base + owner_z(n), n))

    basis = basis_ref[0, 0]
    scal = scal_ref[0]
    stack[...] = jnp.zeros_like(stack)
    for c in range(3):
        stack[32 * c : 32 * c + PC] = basis.astype(f32)
    for c, term in enumerate(split3(scal)):
        stack[96 + c : 97 + c] = term.astype(f32)
    stack[99:100] = scal
    for i in range(NI // 128):
        ext[128 * i : 128 * i + 128] = stack[:, 128 * i : 128 * i + 128].T
    load.wait()
    wgt[...] = (ext[:, 99:100] * res[...].astype(f32)).astype(bf16)
    primal = nn(basis, wgt[...])

    pm = jnp.broadcast_to(pmap_ref[0].astype(f32), (PC, PC))
    map_col = jnp.sum(jnp.where(iota((PC, PC), 0) == iota((PC, PC), 1), pm, 0.0), axis=1, keepdims=True)
    lane = iota((8, 128), 1)
    map_tile = jnp.zeros((8, 128), f32)
    for a in range(3):
        map_tile = jnp.where(lane == 96 + a, map_col[8 * a : 8 * a + 8], map_tile)
    for half in range(2):
        for m in range(4):
            tile = map_tile
            for a in range(3):
                piece = primal[8 * a : 8 * a + 8, 128 * half : 128 * half + 128]
                shift = 32 * ((a - m) % 4)
                if shift:
                    piece = pltpu.roll(piece, shift, 1)
                tile = jnp.where(lane // 32 == a, piece, tile)
            tiles[4 * half + m] = tile

    pl.semaphore_wait(barrier, (NN - 1) + 2 + NN + 9 * is_owner.astype(jnp.int32))

    def owned(c):
        return jnp.logical_and(is_owner, c == n)

    def deliver(src, dst, send, recv, device, here):
        @pl.when(here)
        def _():
            pltpu.make_async_copy(src, dst, recv).start()

        @pl.when(jnp.logical_not(here))
        def _():
            pltpu.make_async_remote_copy(
                src_ref=src, dst_ref=dst, send_sem=send, recv_sem=recv, device_id=device, device_id_type=MESH
            ).start()

    def sent(src, dst, send, recv, device, here):
        @pl.when(jnp.logical_not(here))
        def _():
            pltpu.make_async_remote_copy(
                src_ref=src, dst_ref=dst, send_sem=send, recv_sem=recv, device_id=device, device_id_type=MESH
            ).wait_send()

    piece_at = pl.ds(pl.multiple_of(n * PIECE, 8), PIECE)

    def prim_args(c):
        return (tiles.at[c], prim_in.at[z * NN + n], prim_send.at[c], prim_recv, (base + owner_z(c), c), owned(c))

    def sub_args(c):
        return (sub_hbm.at[0, piece_at], sub.at[z, piece_at], sub_send.at[c], sub_recv.at[z], (base + owner_z(c), c), owned(c))

    def piv_args(c):
        return (piv_hbm.at[0, piece_at], piv.at[z, piece_at], piv_send.at[c], piv_recv, (base + owner_z(c), c), owned(c))

    def map_copy(c):
        return pltpu.make_async_remote_copy(
            src_ref=tiles.at[0], dst_ref=maps.at[n], send_sem=map_send.at[c], recv_sem=map_recv.at[n],
            device_id=(w, c), device_id_type=MESH,
        )

    def in_map(c):
        return pltpu.make_async_copy(maps.at[c], maps.at[c], map_recv.at[c])

    for args in (prim_args, sub_args):
        @pl.loop(0, NN)
        def _(c, args=args):
            deliver(*args(c))

    @pl.loop(0, NN)
    def _(c):
        deliver(*piv_args(c))

        @pl.when(c != n)
        def _():
            map_copy(c).start()

    maps[n] = tiles[0]

    rows[:, 512:640] = ext[...].astype(bf16)

    @pl.loop(0, NI // TILE)
    def _(i):
        at = pl.ds(pl.multiple_of(i * TILE, TILE), TILE)
        inv_load(i).wait()
        part = nn(inv[at], wgt[...])
        local[at] = part
        high, low = split2(part)
        rows[at, 0:256] = high
        rows[at, 256:512] = low

    slot_lane = iota((1, TILE), 1)
    for k in range(NS):
        idxm[k : k + 1] = jnp.where(slot_lane < slen_ref[0, 0, k], sidx_ref[0, 0, k : k + 1], -1)

    def pick_copy(k):
        to_w = jnp.where(k == 8, below, jnp.where(k == 9, above, w))
        to_n = jnp.where(k < 8, k, n)
        slot = jnp.where(k == 8, 9, jnp.where(k == 9, 8, n))
        return pltpu.make_async_remote_copy(
            src_ref=pick_out.at[k], dst_ref=pick_in.at[slot], send_sem=pick_send.at[k], recv_sem=pick_recv.at[slot],
            device_id=(to_w, to_n), device_id_type=MESH,
        )

    def in_pick(k):
        return pltpu.make_async_copy(pick_in.at[k], pick_in.at[k], pick_recv.at[k])

    @pl.loop(0, NS)
    def _(k):
        @pl.when(k != n)
        def _():
            row = jnp.broadcast_to(idxm[pl.ds(k, 1)].astype(f32), (TILE, TILE))
            col = jnp.sum(jnp.where(iota((TILE, TILE), 0) == iota((TILE, TILE), 1), row, 0.0), axis=1, keepdims=True)
            hot = jnp.where(col.astype(jnp.int32) == iota((TILE, NI), 1), 1.0, 0.0).astype(bf16)
            pick_out[k] = nn(hot, rows[...]).astype(bf16)
            pick_copy(k).start()

    def y_copies(d):
        device = (lax.rem(y + d, NY) * NZ + z, n)
        return [
            pltpu.make_async_remote_copy(
                src_ref=chain.at[NZ - 1, part], dst_ref=planes.at[y, part], send_sem=send.at[d - 1], recv_sem=recv.at[y],
                device_id=device, device_id_type=MESH,
            )
            for part, send, recv in ((pl.ds(0, CH), y_send, y_recv), (pl.ds(CH, G), t_send, t_recv))
        ]

    def back_copy(d):
        return pltpu.make_async_remote_copy(
            src_ref=xplanes.at[y], dst_ref=xplanes.at[y], send_sem=b_send.at[d - 1], recv_sem=b_recv.at[y],
            device_id=(lax.rem(y + d, NY) * NZ + z, n), device_id_type=MESH,
        )

    chunk_at = pl.ds(pl.multiple_of(n * CH, CH), CH)

    def x_args(v):
        return (xs.at[v], xfull.at[chunk_at], x_send.at[v], x_recv, (base + v, n), v == z)

    @pl.when(is_owner)
    def _():
        pltpu.make_async_copy(prim_in, prim_in, prim_recv).wait()

        @pl.loop(0, NZ)
        def _(v):
            hots = []
            for c in range(NN):
                tile = prim_in[v * NN + c]
                for a in range(3):
                    at = PC * c + 8 * a
                    prim_v[at : at + 8] = pltpu.roll(tile, 128 - 32 * a, 1) if a else tile
                    col = tile[:, 96 + a : 97 + a].astype(jnp.int32)
                    hots.append(jnp.where(col == iota((8, G), 1), 1.0, 0.0))
            hot = jnp.concatenate(hots, axis=0).astype(bf16)
            high, middle, low = split3(prim_v[...].T[:CH])
            rhs[v] = nn(high, hot) + (nn(middle, hot) + nn(low, hot))

        def in_sub(v):
            pltpu.make_async_copy(sub.at[v], sub.at[v], sub_recv.at[v]).wait()

        eye = jnp.where(iota((G, G), 0) == iota((G, G), 1), 1.0, 0.0)
        in_sub(0)
        chain[0, 0:CH] = rhs[0]
        first_high, first_low = split2(sub[0])
        chain[0, CH:CARRY] = -(nt(eye.astype(bf16), first_high) + nt(eye.astype(bf16), first_low))

        @pl.loop(1, NZ)
        def _(v):
            in_sub(v)
            step = dot3(nt, chain[v - 1], sub[v])
            chain[v, 0:CH] = rhs[v] - step[0:CH]
            chain[v, CH:CARRY] = -step[CH:CARRY]

        for d in range(1, NY):
            y_copies(d)[0].start()
        for d in range(1, NY):
            y_copies(d)[1].start()
        planes[y] = chain[NZ - 1]
        high_carry[NZ - 1] = -eye

        @pl.loop(0, NZ - 1)
        def _(i):
            v = NZ - 2 - i
            high_carry[v] = -dot3(nn, high_carry[v + 1], sub[v + 1])

        pltpu.make_async_copy(piv, piv, piv_recv).wait()

    @pl.loop(0, NI // TILE)
    def _(i):
        at = pl.ds(pl.multiple_of(i * TILE, TILE), TILE)
        row_id = iota((TILE, TILE), 0) + i * TILE
        for k in range(NS):
            select[at, TILE * k : TILE * k + TILE] = jnp.where(idxm[k : k + 1] == row_id, 1.0, 0.0).astype(bf16)

    @pl.loop(0, NN)
    def _(c):
        @pl.when(c != n)
        def _():
            in_map(c).wait()

    for c in range(NN):
        tile = maps[c]
        for a in range(3):
            col = tile[:, 96 + a : 97 + a].astype(jnp.int32)
            spread_map[32 * c + 8 * a : 32 * c + 8 * a + 8] = jnp.where(col == iota((8, G), 1), 1.0, 0.0)
        spread_map[32 * c + PC : 32 * c + 32] = jnp.zeros((32 - PC, G), f32)
    vals[:, 96:128] = jnp.zeros((NS, 32, R), bf16)

    @pl.when(is_owner)
    def _():
        def in_plane(d):
            src = lax.rem(y + NY - d, NY)
            for part, recv in ((pl.ds(0, CH), y_recv), (pl.ds(CH, G), t_recv)):
                pltpu.make_async_copy(planes.at[src, part], planes.at[src, part], recv.at[src]).wait()

        for d in range(1, NY):
            in_plane(d)
        carry[...] = jnp.where(y > 0, planes[0, 0:CH], 0.0)
        for g in range(1, NY - 1):
            @pl.when(y > g)
            def _(g=g):
                carry[...] = planes[g, 0:CH] + dot3(nn, carry[...], planes[g, CH:CARRY])

        for v in range(NZ):
            solved = chain[v, 0:CH] + dot3(nn, carry[...], chain[v, CH:CARRY])
            pivoted[v] = dot3(nn, solved, piv[v])
        xs[NZ - 1] = pivoted[NZ - 1]

        @pl.loop(0, NZ - 1)
        def _(i):
            v = NZ - 2 - i
            xs[v] = pivoted[v] - dot3(nn, xs[v + 1], sub[v + 1])

        xplanes[y] = dot3(nn, xs[0], sub[0])
        for d in range(1, NY):
            back_copy(d).start()
        for d in range(1, NY):
            src = lax.rem(y + NY - d, NY)
            pltpu.make_async_copy(xplanes.at[src], xplanes.at[src], b_recv.at[src]).wait()
        carry[...] = jnp.where(y < NY - 1, xplanes[NY - 1], 0.0)
        for g in range(NY - 2, 0, -1):
            @pl.when(y < g)
            def _(g=g):
                carry[...] = xplanes[g] + dot3(nt, carry[...], planes[g, CH:CARRY])

        for v in range(NZ):
            xs[v] = xs[v] + dot3(nn, carry[...], high_carry[v])

        @pl.loop(0, NZ)
        def _(v):
            deliver(*x_args(v))

    def gather_copy(c):
        return pltpu.make_async_remote_copy(
            src_ref=xfull.at[chunk_at], dst_ref=xfull.at[chunk_at], send_sem=gather_send.at[c], recv_sem=gather_recv.at[n],
            device_id=(w, c), device_id_type=MESH,
        )

    pltpu.make_async_copy(xfull.at[chunk_at], xfull.at[chunk_at], x_recv).wait()

    @pl.loop(1, NN)
    def _(d):
        gather_copy(lax.rem(n + d, NN)).start()

    @pl.loop(1, NN)
    def _(d):
        src = lax.rem(n + d, NN)
        at = pl.ds(pl.multiple_of(src * CH, CH), CH)
        pltpu.make_async_copy(xfull.at[at], xfull.at[at], gather_recv.at[src]).wait()

    hot = spread_map[...].astype(bf16)
    for c, term in enumerate(split3(xfull[...])):
        picked = nt(hot, term).astype(bf16)
        for j in range(NN):
            vals[j, 32 * c : 32 * c + 32] = picked[32 * j : 32 * j + 32]

    def val_copy(side):
        return pltpu.make_async_remote_copy(
            src_ref=vals.at[n, pl.ds(0, 96)], dst_ref=vals.at[8 + side, pl.ds(0, 96)],
            send_sem=val_send.at[side], recv_sem=val_recv.at[side],
            device_id=(above if side == 0 else below, n), device_id_type=MESH,
        )

    for side in range(2):
        val_copy(side).start()

    def receive(k):
        in_pick(k).wait()
        picked = pick_in[k]
        spread = nn(picked[:, 512:640], vals[k])
        weight = jnp.sum(picked[:, 608:611].astype(f32), axis=1, keepdims=True)
        part = picked[:, 0:256].astype(f32) + picked[:, 256:512].astype(f32)
        at = pl.ds(pl.multiple_of(k * TILE, TILE), TILE)
        inc[at] = (weight * (part + spread)).astype(bf16)

    @pl.loop(0, NN)
    def _(k):
        @pl.when(k != n)
        def _():
            receive(k)

    own_at = pl.ds(pl.multiple_of(n * TILE, TILE), TILE)
    inc[own_at] = jnp.zeros((TILE, R), bf16)

    @pl.loop(0, NI // TILE)
    def _(i):
        at = pl.ds(pl.multiple_of(i * TILE, TILE), TILE)
        spread = nn(rows[at, 512:640], vals[n])
        combined = (ext[at, 99:100] * (local[at] + spread)).astype(bf16)
        result[at] = combined.astype(f32)

    for side in range(2):
        into = vals.at[8 + side, pl.ds(0, 96)]
        pltpu.make_async_copy(into, into, val_recv.at[side]).wait()
        receive(8 + side)

    def store(i):
        at = pl.ds(pl.multiple_of(i * TILE, TILE), TILE)
        return pltpu.make_async_copy(result.at[at], out_hbm.at[0, 0, at], out_sem.at[i])

    @pl.loop(0, NI // TILE)
    def _(i):
        at = pl.ds(pl.multiple_of(i * TILE, TILE), TILE)
        result[at] += nn(select[at], inc[...])
        store(i).start()

    @pl.loop(0, NN)
    def _(c):
        sent(*prim_args(c))
        sent(*sub_args(c))
        sent(*piv_args(c))

        @pl.when(c != n)
        def _():
            map_copy(c).wait_send()
            gather_copy(c).wait_send()

    @pl.loop(0, NS)
    def _(k):
        @pl.when(k != n)
        def _():
            pick_copy(k).wait_send()

    for side in range(2):
        val_copy(side).wait_send()

    @pl.when(is_owner)
    def _():
        for d in range(1, NY):
            for copy in y_copies(d):
                copy.wait_send()
            back_copy(d).wait_send()

        @pl.loop(0, NZ)
        def _(v):
            sent(*x_args(v))

    @pl.loop(0, NI // TILE)
    def _(i):
        store(i).wait()


def body(residual, scaling, inverse, basis, primal_map, slot_index, slot_length, sub, pivot):
    vmem = pl.BlockSpec(memory_space=pltpu.VMEM)
    smem = pl.BlockSpec(memory_space=pltpu.SMEM)
    hbm = pl.BlockSpec(memory_space=pl.ANY)
    dma = pltpu.SemaphoreType.DMA
    V = pltpu.VMEM
    return pl.pallas_call(
        kernel,
        out_shape=jax.ShapeDtypeStruct((1, 1, NI, R), f32),
        in_specs=[hbm, vmem, hbm, vmem, vmem, vmem, smem, hbm, hbm],
        out_specs=hbm,
        scratch_shapes=[
            V((NI, R), bf16), V((NI, NI), bf16), V((NI, R), bf16), V((NI, R), f32), V((NI, 640), bf16), V((NI, 128), f32),
            V((NI, NS * TILE), bf16), V((NS, TILE, 640), bf16), V((NS, TILE, 640), bf16), V((NS * TILE, R), bf16), V((NI, R), f32),
            V((16, TILE), jnp.int32), V((NN, 8, 128), f32), V((NN, 8, 128), f32), V((NN * 32, G), f32), V((NS, 128, R), bf16),
            V((R, G), f32), V((128, NI), f32),
            V((NZ * NN, 8, 128), f32), V((G, 128), f32), V((NZ, G, G), f32), V((NZ, G, G), f32), V((NZ, CARRY, G), f32),
            V((NZ, CH, G), f32), V((NY, CARRY, G), f32), V((NZ, G, G), f32), V((NZ, CH, G), f32), V((NZ, CH, G), f32),
            V((NY, CH, G), f32), V((CH, G), f32),
            dma, dma((NI // TILE,)), dma((NI // TILE,)),
            dma((NN,)), dma, dma((NN,)), dma((NZ,)), dma((NN,)), dma,
            dma((NN,)), dma((NN,)), dma((NS,)), dma((NS,)),
            dma((NY - 1,)), dma((NY,)), dma((NY - 1,)), dma((NY,)), dma((NY - 1,)), dma((NY,)),
            dma((NZ,)), dma, dma((NN,)), dma((NN,)), dma((2,)), dma((2,)),
        ],
        compiler_params=pltpu.CompilerParams(collective_id=0, has_side_effects=True, vmem_limit_bytes=58 * 2**20),
    )(residual, scaling, inverse, basis, primal_map, slot_index, slot_length, sub, pivot)


def solution(mesh):
    in_specs = (
        P("wide", "narrow", None, None),
        P("wide", "narrow", None),
        P("wide", "narrow", None, None),
        P("wide", "narrow", None, None),
        P("wide", "narrow", None),
        P("wide", "narrow", None, None),
        P("wide", "narrow", None),
        P("wide", None, None),
        P("wide", None, None),
    )
    out_specs = P("wide", "narrow", None, None)
    return jax.shard_map(body, mesh=mesh, in_specs=in_specs, out_specs=out_specs, check_vma=False)
```

```python
import jax
import jax.numpy as jnp
from jax import lax
from jax.experimental import pallas as pl
from jax.experimental.pallas import tpu as pltpu
from jax.sharding import PartitionSpec as P

MESH = pl.DeviceIdType.MESH
f32 = jnp.float32
bf16 = jnp.bfloat16
NZ = 8
NY = 4
NN = 8
NS = 10
NI = 2048
R = 256
PC = 24
G = 192
CH = R // NN
PIECE = G // NN
PIVOT_PIECE = 32
CARRY = CH + G
TILE = 256
HALF = 512
PACK = TILE // 8
EARLY = 4


def owner_z(n):
    return n // 2 + 4 * (n % 2)


def iota(shape, axis):
    return lax.broadcasted_iota(jnp.int32, shape, axis)


def split2(a):
    high = a.astype(bf16)
    return high, (a - high.astype(f32)).astype(bf16)


def split3(a):
    high = a.astype(bf16)
    rest = a - high.astype(f32)
    middle = rest.astype(bf16)
    return high, middle, (rest - middle.astype(f32)).astype(bf16)


def nn(a, b):
    return lax.dot_general(a, b, (((1,), (0,)), ((), ())), preferred_element_type=f32)


def nt(a, b):
    return lax.dot_general(a, b, (((1,), (1,)), ((), ())), preferred_element_type=f32)


def dot3(dot, a, b):
    a_high, a_low = split2(a)
    b_high, b_low = split2(b)
    return dot(a_high, b_high) + (dot(a_high, b_low) + dot(a_low, b_high))


def kernel(
    res_hbm, scal_ref, inv_hbm, basis_ref, pmap_ref, sidx_ref, slen_ref, sub_hbm, piv_hbm,
    out_hbm,
    res, inv, wgt, local, rows, ext, select, pick_out, pick_in, inc, result,
    part_in, ext_in, weight_in, own_ext, pivot_rows, pivot_out,
    idxm, tiles, maps, spread_map, vals, xfull, stack,
    prim_in, prim_v, sub, piv, chain, rhs, planes, high_carry, pivoted, xs, xplanes, carry,
    load_sem, pivot_sem, inv_sem, out_sem,
    prim_send, prim_recv, sub_send, sub_recv, piv_send, piv_recv,
    map_send, map_recv, pick_send, pick_recv,
    y_send, y_recv, t_send, t_recv, b_send, b_recv,
    x_send, x_recv, gather_send, gather_recv, val_send, val_recv, go_sem,
):
    w = lax.axis_index("wide")
    n = lax.axis_index("narrow")
    y = w // NZ
    z = w % NZ
    base = y * NZ
    above = lax.rem(w + 1, NY * NZ)
    below = lax.rem(w + NY * NZ - 1, NY * NZ)
    is_owner = z == owner_z(n)
    inner = jnp.logical_and(y > 0, y < NY - 1)

    load = pltpu.make_async_copy(res_hbm.at[0, 0], res, load_sem)
    load.start()
    pivot_at = pl.ds(pl.multiple_of(PIVOT_PIECE * jnp.minimum(n, 5), PIVOT_PIECE), PIVOT_PIECE)
    pivot_load = pltpu.make_async_copy(piv_hbm.at[0, pivot_at], pivot_rows, pivot_sem)
    pivot_load.start()

    def inv_load(i):
        at = pl.ds(pl.multiple_of(i * HALF, HALF), HALF)
        return pltpu.make_async_copy(inv_hbm.at[0, 0, at], inv.at[at], inv_sem.at[i])

    @pl.loop(0, NI // HALF)
    def _(i):
        inv_load(i).start()

    barrier = pltpu.get_barrier_semaphore()

    def hello(device):
        pl.semaphore_signal(barrier, inc=1, device_id=device, device_id_type=MESH)

    for d in range(1, NN):
        hello((w, lax.rem(n + d, NN)))
    hello((above, n))
    hello((below, n))

    @pl.when(is_owner)
    def _():
        @pl.loop(0, NZ)
        def _(v):
            for c in range(NN):
                @pl.when(jnp.logical_or(v != z, c != n))
                def _(c=c):
                    hello((base + v, c))

        for d in range(1, NY):
            hello((lax.rem(y + d, NY) * NZ + z, n))

    @pl.when(jnp.logical_not(is_owner))
    def _():
        hello((base + owner_z(n), n))

    basis = basis_ref[0, 0]
    scal = scal_ref[0]
    stack[...] = jnp.zeros_like(stack)
    for c in range(3):
        stack[32 * c : 32 * c + PC] = basis.astype(f32)
    for c, term in enumerate(split3(scal)):
        stack[PC + c : PC + c + 1] = term.astype(f32)
    stack[27:28] = scal
    for i in range(NI // 128):
        ext[128 * i : 128 * i + 128] = stack[:, 128 * i : 128 * i + 128].T
    load.wait()
    wgt[...] = (ext[:, 27:28] * res[...].astype(f32)).astype(bf16)
    primal = nn(basis, wgt[...])

    pm = jnp.broadcast_to(pmap_ref[0].astype(f32), (PC, PC))
    map_col = jnp.sum(jnp.where(iota((PC, PC), 0) == iota((PC, PC), 1), pm, 0.0), axis=1, keepdims=True)
    lane = iota((8, 128), 1)
    map_tile = jnp.zeros((8, 128), f32)
    for a in range(3):
        map_tile = jnp.where(lane == 96 + a, map_col[8 * a : 8 * a + 8], map_tile)
    for half in range(2):
        for m in range(4):
            tile = map_tile
            for a in range(3):
                piece = primal[8 * a : 8 * a + 8, 128 * half : 128 * half + 128]
                shift = 32 * ((a - m) % 4)
                if shift:
                    piece = pltpu.roll(piece, shift, 1)
                tile = jnp.where(lane // 32 == a, piece, tile)
            tiles[4 * half + m] = tile

    pl.semaphore_wait(barrier, (NN - 1) + 2 + NN + 9 * is_owner.astype(jnp.int32))

    def owned(c):
        return jnp.logical_and(is_owner, c == n)

    def turn(i):
        return lax.rem(i + n + z, NN)

    def deliver(src, dst, send, recv, device, here):
        @pl.when(here)
        def _():
            pltpu.make_async_copy(src, dst, recv).start()

        @pl.when(jnp.logical_not(here))
        def _():
            pltpu.make_async_remote_copy(
                src_ref=src, dst_ref=dst, send_sem=send, recv_sem=recv, device_id=device, device_id_type=MESH
            ).start()

    def sent(src, dst, send, recv, device, here):
        @pl.when(jnp.logical_not(here))
        def _():
            pltpu.make_async_remote_copy(
                src_ref=src, dst_ref=dst, send_sem=send, recv_sem=recv, device_id=device, device_id_type=MESH
            ).wait_send()

    piece_at = pl.ds(pl.multiple_of(n * PIECE, 8), PIECE)

    def prim_args(c):
        return (tiles.at[c], prim_in.at[z * NN + n], prim_send.at[c], prim_recv, (base + owner_z(c), c), owned(c))

    def sub_args(c):
        return (sub_hbm.at[0, piece_at], sub.at[z, piece_at], sub_send.at[c], sub_recv.at[z], (base + owner_z(c), c), owned(c))

    def piv_args(c):
        return (pivot_out, piv.at[z, pivot_at], piv_send.at[c], piv_recv, (base + owner_z(c), c), owned(c))

    def map_copy(c):
        return pltpu.make_async_remote_copy(
            src_ref=tiles.at[0], dst_ref=maps.at[n], send_sem=map_send.at[c], recv_sem=map_recv.at[n],
            device_id=(w, c), device_id_type=MESH,
        )

    def in_map(c):
        return pltpu.make_async_copy(maps.at[c], maps.at[c], map_recv.at[c])

    @pl.loop(0, NN)
    def _(i):
        deliver(*prim_args(turn(i)))

    @pl.loop(0, NN)
    def _(i):
        deliver(*sub_args(turn(i)))

    @pl.loop(0, NN)
    def _(i):
        c = turn(i)

        @pl.when(c != n)
        def _():
            map_copy(c).start()

    maps[n] = tiles[0]

    own_ext[...] = ext[...].astype(bf16)
    rows[:, 256:384] = jnp.where(iota((NI, 128), 1) < 32, ext[...], 0.0).astype(bf16)

    @pl.loop(0, NI // HALF)
    def _(i):
        at = pl.ds(pl.multiple_of(i * HALF, HALF), HALF)
        inv_load(i).wait()
        part = nn(inv[at], wgt[...])
        local[at] = part
        rows[at, 0:256] = part.astype(bf16)

    slot_lane = iota((1, TILE), 1)
    for k in range(NS):
        idxm[k : k + 1] = jnp.where(slot_lane < slen_ref[0, 0, k], sidx_ref[0, k], -1)

    @pl.loop(0, NI // TILE)
    def _(i):
        at = pl.ds(pl.multiple_of(i * TILE, TILE), TILE)
        row_id = iota((TILE, TILE), 0) + i * TILE
        for k in range(NS):
            select[at, TILE * k : TILE * k + TILE] = jnp.where(idxm[k : k + 1] == row_id, 1.0, 0.0).astype(bf16)

    pivot_load.wait()
    pivot_out[...] = pivot_rows[...].astype(bf16)

    @pl.when(n < G // PIVOT_PIECE)
    def _():
        @pl.loop(0, NN)
        def _(i):
            deliver(*piv_args(turn(i)))

    def pick_copy(k):
        to_w = jnp.where(k == 8, below, jnp.where(k == 9, above, w))
        to_n = jnp.where(k < 8, k, n)
        slot = jnp.where(k == 8, 9, jnp.where(k == 9, 8, n))
        return pltpu.make_async_remote_copy(
            src_ref=pick_out.at[k], dst_ref=pick_in.at[slot], send_sem=pick_send.at[k], recv_sem=pick_recv.at[slot],
            device_id=(to_w, to_n), device_id_type=MESH,
        )

    def in_pick(k):
        return pltpu.make_async_copy(pick_in.at[k], pick_in.at[k], pick_recv.at[k])

    def slot_at(i):
        return jnp.where(i < NN - 1, lax.rem(n + i + 1, NN), i + 1)

    def pick(i):
        k = slot_at(i)
        row = jnp.broadcast_to(idxm[pl.ds(k, 1)].astype(f32), (TILE, TILE))
        col = jnp.sum(jnp.where(iota((TILE, TILE), 0) == iota((TILE, TILE), 1), row, 0.0), axis=1, keepdims=True)
        hot = jnp.where(col.astype(jnp.int32) == iota((TILE, NI), 1), 1.0, 0.0).astype(bf16)
        picked = nn(hot, rows[...])
        pick_out[k, 0:TILE] = picked[:, 0:256].astype(bf16)
        for g in range(2):
            packed = picked[PACK * 4 * g : PACK * 4 * g + PACK, 256:384]
            for q in range(1, 4):
                at = PACK * (4 * g + q)
                packed = packed + pltpu.roll(picked[at : at + PACK, 256:384], 32 * q, 1)
            pick_out[k, TILE : TILE + PACK, 128 * g : 128 * g + 128] = packed.astype(bf16)

    pl.loop(0, jnp.where(is_owner, EARLY, NS - 1))(pick)

    def send_picks(first, last):
        @pl.loop(first, last)
        def _(i):
            pick_copy(slot_at(i)).start()

    @pl.when(jnp.logical_not(is_owner))
    def _():
        pl.semaphore_wait(go_sem, 1)
        send_picks(0, NS - 1)

    def y_copies(d):
        device = (lax.rem(y + d, NY) * NZ + z, n)
        return [
            pltpu.make_async_remote_copy(
                src_ref=chain.at[NZ - 1, part], dst_ref=planes.at[y, part], send_sem=send.at[d - 1], recv_sem=recv.at[y],
                device_id=device, device_id_type=MESH,
            )
            for part, send, recv in ((pl.ds(0, CH), y_send, y_recv), (pl.ds(CH, G), t_send, t_recv))
        ]

    def back_copy(d):
        return pltpu.make_async_remote_copy(
            src_ref=xplanes.at[y], dst_ref=xplanes.at[y], send_sem=b_send.at[d - 1], recv_sem=b_recv.at[y],
            device_id=(lax.rem(y + d, NY) * NZ + z, n), device_id_type=MESH,
        )

    chunk_at = pl.ds(pl.multiple_of(n * CH, CH), CH)

    def x_args(v):
        return (xs.at[v], xfull.at[chunk_at], x_send.at[v], x_recv, (base + v, n), v == z)

    @pl.when(is_owner)
    def _():
        pltpu.make_async_copy(prim_in, prim_in, prim_recv).wait()

        @pl.loop(0, NZ)
        def _(v):
            hots = []
            for c in range(NN):
                tile = prim_in[v * NN + c]
                for a in range(3):
                    at = PC * c + 8 * a
                    prim_v[at : at + 8] = pltpu.roll(tile, 128 - 32 * a, 1) if a else tile
                    col = tile[:, 96 + a : 97 + a].astype(jnp.int32)
                    hots.append(jnp.where(col == iota((8, G), 1), 1.0, 0.0))
            hot = jnp.concatenate(hots, axis=0).astype(bf16)
            high, middle, low = split3(prim_v[...].T[:CH])
            rhs[v] = nn(high, hot) + (nn(middle, hot) + nn(low, hot))

        def in_sub(v):
            pltpu.make_async_copy(sub.at[v], sub.at[v], sub_recv.at[v]).wait()

        for v in range(NZ):
            in_sub(v)

        @pl.loop(0, NZ)
        def _(v):
            @pl.when(v != z)
            def _():
                pl.semaphore_signal(go_sem, inc=1, device_id=(base + v, n), device_id_type=MESH)

        eye = jnp.where(iota((G, G), 0) == iota((G, G), 1), 1.0, 0.0)
        chain[0, 0:CH] = rhs[0]
        first_high, first_low = split2(sub[0])
        chain[0, CH:CARRY] = -(nt(eye.astype(bf16), first_high) + nt(eye.astype(bf16), first_low))

        @pl.loop(1, NZ)
        def _(v):
            step = dot3(nt, chain[v - 1], sub[v])
            chain[v, 0:CH] = rhs[v] - step[0:CH]
            chain[v, CH:CARRY] = -step[CH:CARRY]

        for d in range(1, NY):
            y_copies(d)[0].start()

        @pl.when(inner)
        def _():
            for d in range(1, NY):
                y_copies(d)[1].start()

        planes[y] = chain[NZ - 1]

        send_picks(0, EARLY)

    pl.loop(jnp.where(is_owner, EARLY, NS - 1), NS - 1)(pick)

    @pl.when(is_owner)
    def _():
        send_picks(EARLY, NS - 1)
        high_carry[NZ - 1] = -jnp.where(iota((G, G), 0) == iota((G, G), 1), 1.0, 0.0)

        @pl.loop(0, NZ - 1)
        def _(i):
            v = NZ - 2 - i
            high_carry[v] = -dot3(nn, high_carry[v + 1], sub[v + 1])

        pltpu.make_async_copy(piv, piv, piv_recv).wait()

    @pl.when(is_owner)
    def _():
        def in_plane(d):
            src = lax.rem(y + NY - d, NY)
            values = planes.at[src, pl.ds(0, CH)]
            pltpu.make_async_copy(values, values, y_recv.at[src]).wait()

            @pl.when(jnp.logical_and(src > 0, src < NY - 1))
            def _():
                product = planes.at[src, pl.ds(CH, G)]
                pltpu.make_async_copy(product, product, t_recv.at[src]).wait()


        for d in range(1, NY):
            in_plane(d)
        carry[...] = jnp.where(y > 0, planes[0, 0:CH], 0.0)
        for g in range(1, NY - 1):
            @pl.when(y > g)
            def _(g=g):
                carry[...] = planes[g, 0:CH] + dot3(nn, carry[...], planes[g, CH:CARRY])

        for v in range(NZ):
            solved = chain[v, 0:CH] + dot3(nn, carry[...], chain[v, CH:CARRY])
            high, low = split2(solved)
            pivoted[v] = nn(high, piv[v]) + nn(low, piv[v])
        xs[NZ - 1] = pivoted[NZ - 1]

        @pl.loop(0, NZ - 1)
        def _(i):
            v = NZ - 2 - i
            xs[v] = pivoted[v] - dot3(nn, xs[v + 1], sub[v + 1])

        xplanes[y] = dot3(nn, xs[0], sub[0])
        for d in range(1, NY):
            back_copy(d).start()
        for d in range(1, NY):
            src = lax.rem(y + NY - d, NY)
            pltpu.make_async_copy(xplanes.at[src], xplanes.at[src], b_recv.at[src]).wait()
        carry[...] = jnp.where(y < NY - 1, xplanes[NY - 1], 0.0)
        for g in range(NY - 2, 0, -1):
            @pl.when(y < g)
            def _(g=g):
                carry[...] = xplanes[g] + dot3(nt, carry[...], planes[g, CH:CARRY])

        for v in range(NZ):
            xs[v] = xs[v] + dot3(nn, carry[...], high_carry[v])

        @pl.loop(0, NZ)
        def _(v):
            deliver(*x_args(v))

    def gather_copy(c):
        return pltpu.make_async_remote_copy(
            src_ref=xfull.at[chunk_at], dst_ref=xfull.at[chunk_at], send_sem=gather_send.at[c], recv_sem=gather_recv.at[n],
            device_id=(w, c), device_id_type=MESH,
        )

    pltpu.make_async_copy(xfull.at[chunk_at], xfull.at[chunk_at], x_recv).wait()

    @pl.loop(1, NN)
    def _(d):
        gather_copy(lax.rem(n + d, NN)).start()

    @pl.loop(0, NN)
    def _(c):
        @pl.when(c != n)
        def _():
            in_map(c).wait()

    for c in range(NN):
        tile = maps[c]
        for a in range(3):
            col = tile[:, 96 + a : 97 + a].astype(jnp.int32)
            spread_map[32 * c + 8 * a : 32 * c + 8 * a + 8] = jnp.where(col == iota((8, G), 1), 1.0, 0.0)
        spread_map[32 * c + PC : 32 * c + 32] = jnp.zeros((32 - PC, G), f32)
    vals[:, 96:128] = jnp.zeros((NS, 32, R), bf16)

    @pl.loop(0, NS)
    def _(k):
        at = pl.ds(pl.multiple_of(k * TILE, TILE), TILE)

        @pl.when(k == n)
        def _():
            part_in[at] = jnp.zeros((TILE, R), f32)
            ext_in[at] = jnp.zeros((TILE, 128), bf16)
            weight_in[at] = jnp.zeros((TILE, 128), f32)

        @pl.when(k != n)
        def _():
            in_pick(k).wait()
            pieces = []
            packed = pick_in[k, TILE : TILE + PACK].astype(f32)
            for q in range(8):
                piece = packed[:, 128 * (q // 4) : 128 * (q // 4) + 128]
                pieces.append(pltpu.roll(piece, 128 - 32 * (q % 4), 1) if q % 4 else piece)
            extra = jnp.where(iota((TILE, 128), 1) < 32, jnp.concatenate(pieces, axis=0), 0.0)
            weight = extra[:, PC : PC + 1] + extra[:, PC + 1 : PC + 2] + extra[:, PC + 2 : PC + 3]
            ext_in[at] = (extra + (pltpu.roll(extra, 32, 1) + pltpu.roll(extra, 64, 1))).astype(bf16)
            weight_in[at] = jnp.broadcast_to(weight, (TILE, 128))
            part_in[at] = weight * pick_in[k, 0:TILE].astype(f32)

    @pl.loop(1, NN)
    def _(d):
        src = lax.rem(n + d, NN)
        at = pl.ds(pl.multiple_of(src * CH, CH), CH)
        pltpu.make_async_copy(xfull.at[at], xfull.at[at], gather_recv.at[src]).wait()

    hot = spread_map[...].astype(bf16)
    for c, term in enumerate(split3(xfull[...])):
        picked = nt(hot, term).astype(bf16)
        for j in range(NN):
            vals[j, 32 * c : 32 * c + 32] = picked[32 * j : 32 * j + 32]

    def val_copy(side):
        return pltpu.make_async_remote_copy(
            src_ref=vals.at[n, pl.ds(0, 96)], dst_ref=vals.at[8 + side, pl.ds(0, 96)],
            send_sem=val_send.at[side], recv_sem=val_recv.at[side],
            device_id=(above if side == 0 else below, n), device_id_type=MESH,
        )

    for side in range(2):
        val_copy(side).start()

    def receive(k):
        at = slice(k * TILE, k * TILE + TILE)
        spread = nn(ext_in[at], vals[k])
        weight = weight_in[at]
        for half in (slice(0, 128), slice(128, 256)):
            inc[at, half] = (part_in[at, half] + weight * spread[:, half]).astype(bf16)

    for k in range(NN):
        receive(k)

    @pl.loop(0, NI // HALF)
    def _(i):
        at = pl.ds(pl.multiple_of(i * HALF, HALF), HALF)
        spread = nn(own_ext[at], vals[n])
        combined = (ext[at, 27:28] * (local[at] + spread)).astype(bf16)
        result[at] = combined.astype(f32) + nn(select[at, 0 : NN * TILE], inc[0 : NN * TILE])

    for side in range(2):
        into = vals.at[8 + side, pl.ds(0, 96)]
        pltpu.make_async_copy(into, into, val_recv.at[side]).wait()
        receive(8 + side)

    def store(i):
        at = pl.ds(pl.multiple_of(i * HALF, HALF), HALF)
        return pltpu.make_async_copy(result.at[at], out_hbm.at[0, 0, at], out_sem.at[i])

    @pl.loop(0, NI // HALF)
    def _(i):
        at = pl.ds(pl.multiple_of(i * HALF, HALF), HALF)
        result[at] += nn(select[at, NN * TILE : NS * TILE], inc[NN * TILE : NS * TILE])
        store(i).start()

    @pl.loop(0, NN)
    def _(c):
        sent(*prim_args(c))
        sent(*sub_args(c))

        @pl.when(n < G // PIVOT_PIECE)
        def _():
            sent(*piv_args(c))

        @pl.when(c != n)
        def _():
            map_copy(c).wait_send()
            gather_copy(c).wait_send()

    @pl.loop(0, NS)
    def _(k):
        @pl.when(k != n)
        def _():
            pick_copy(k).wait_send()

    for side in range(2):
        val_copy(side).wait_send()

    @pl.when(is_owner)
    def _():
        for d in range(1, NY):
            y_copies(d)[0].wait_send()
            back_copy(d).wait_send()

        @pl.when(inner)
        def _():
            for d in range(1, NY):
                y_copies(d)[1].wait_send()

        @pl.loop(0, NZ)
        def _(v):
            sent(*x_args(v))

    @pl.loop(0, NI // HALF)
    def _(i):
        store(i).wait()


def body(residual, scaling, inverse, basis, primal_map, slot_index, slot_length, sub, pivot):
    vmem = pl.BlockSpec(memory_space=pltpu.VMEM)
    smem = pl.BlockSpec(memory_space=pltpu.SMEM)
    hbm = pl.BlockSpec(memory_space=pl.ANY)
    dma = pltpu.SemaphoreType.DMA
    V = pltpu.VMEM
    return pl.pallas_call(
        kernel,
        out_shape=jax.ShapeDtypeStruct((1, 1, NI, R), f32),
        in_specs=[hbm, vmem, hbm, vmem, vmem, vmem, smem, hbm, hbm],
        out_specs=hbm,
        scratch_shapes=[
            V((NI, R), bf16), V((NI, NI), bf16), V((NI, R), bf16), V((NI, R), f32), V((NI, 384), bf16), V((NI, 128), f32),
            V((NI, NS * TILE), bf16), V((NS, TILE + PACK, 256), bf16), V((NS, TILE + PACK, 256), bf16), V((NS * TILE, R), bf16),
            V((NI, R), f32), V((NS * TILE, R), f32), V((NS * TILE, 128), bf16), V((NS * TILE, 128), f32), V((NI, 128), bf16),
            V((PIVOT_PIECE, G), f32), V((PIVOT_PIECE, G), bf16),
            V((16, TILE), jnp.int32), V((NN, 8, 128), f32), V((NN, 8, 128), f32), V((NN * 32, G), f32), V((NS, 128, R), bf16),
            V((R, G), f32), V((128, NI), f32),
            V((NZ * NN, 8, 128), f32), V((G, 128), f32), V((NZ, G, G), f32), V((NZ, G, G), bf16), V((NZ, CARRY, G), f32),
            V((NZ, CH, G), f32), V((NY, CARRY, G), f32), V((NZ, G, G), f32), V((NZ, CH, G), f32), V((NZ, CH, G), f32),
            V((NY, CH, G), f32), V((CH, G), f32),
            dma, dma, dma((NI // HALF,)), dma((NI // HALF,)),
            dma((NN,)), dma, dma((NN,)), dma((NZ,)), dma((NN,)), dma,
            dma((NN,)), dma((NN,)), dma((NS,)), dma((NS,)),
            dma((NY - 1,)), dma((NY,)), dma((NY - 1,)), dma((NY,)), dma((NY - 1,)), dma((NY,)),
            dma((NZ,)), dma, dma((NN,)), dma((NN,)), dma((2,)), dma((2,)), pltpu.SemaphoreType.REGULAR,
        ],
        compiler_params=pltpu.CompilerParams(collective_id=0, has_side_effects=True, vmem_limit_bytes=58 * 2**20),
    )(residual, scaling, inverse, basis, primal_map, slot_index.transpose(0, 2, 1, 3), slot_length, sub, pivot)


def solution(mesh):
    in_specs = (
        P("wide", "narrow", None, None),
        P("wide", "narrow", None),
        P("wide", "narrow", None, None),
        P("wide", "narrow", None, None),
        P("wide", "narrow", None),
        P("wide", "narrow", None, None),
        P("wide", "narrow", None),
        P("wide", None, None),
        P("wide", None, None),
    )
    out_specs = P("wide", "narrow", None, None)
    return jax.shard_map(body, mesh=mesh, in_specs=in_specs, out_specs=out_specs, check_vma=False)
```

```python
import jax
import jax.numpy as jnp
from jax import lax
from jax.experimental import pallas as pl
from jax.experimental.pallas import tpu as pltpu
from jax.sharding import PartitionSpec as P

MESH = pl.DeviceIdType.MESH
f32 = jnp.float32
bf16 = jnp.bfloat16
NZ = 8
NY = 4
NN = 8
NS = 10
NI = 2048
R = 256
PC = 24
G = 192
CH = R // NN
PIECE = G // NN
PIVOT_PIECE = 32
CARRY = CH + G
TILE = 256
HALF = 512
PACK = TILE // 8
EARLY = 4


def owner_z(n):
    return n // 2 + 4 * (n % 2)


def iota(shape, axis):
    return lax.broadcasted_iota(jnp.int32, shape, axis)


def split2(a):
    high = a.astype(bf16)
    return high, (a - high.astype(f32)).astype(bf16)


def split3(a):
    high = a.astype(bf16)
    rest = a - high.astype(f32)
    middle = rest.astype(bf16)
    return high, middle, (rest - middle.astype(f32)).astype(bf16)


def nn(a, b):
    return lax.dot_general(a, b, (((1,), (0,)), ((), ())), preferred_element_type=f32)


def nt(a, b):
    return lax.dot_general(a, b, (((1,), (1,)), ((), ())), preferred_element_type=f32)


def dot3(dot, a, b):
    a_high, a_low = split2(a)
    b_high, b_low = split2(b)
    return dot(a_high, b_high) + (dot(a_high, b_low) + dot(a_low, b_high))


def kernel(
    res_hbm, scal_ref, inv_hbm, basis_ref, pmap_ref, sidx_ref, slen_ref, sub_hbm, piv_hbm,
    out_hbm,
    res, inv, wgt, local, rows, ext, select, pick_out, pick_in, inc, result,
    part_in, ext_in, weight_in, own_ext, pivot_rows, pivot_out,
    idxm, tiles, maps, spread_map, vals, xfull, stack,
    prim_in, prim_v, sub, piv, chain, rhs, planes, high_carry, pivoted, xs, xplanes, carry, x_out, product_out, products,
    load_sem, pivot_sem, inv_sem, out_sem,
    prim_send, prim_recv, sub_send, sub_recv, piv_send, piv_recv,
    map_send, map_recv, pick_send, pick_recv,
    y_send, y_recv, t_send, t_recv, b_send, b_recv,
    x_send, x_recv, gather_send, gather_recv, val_send, val_recv, go_sem,
):
    w = lax.axis_index("wide")
    n = lax.axis_index("narrow")
    y = w // NZ
    z = w % NZ
    base = y * NZ
    above = lax.rem(w + 1, NY * NZ)
    below = lax.rem(w + NY * NZ - 1, NY * NZ)
    is_owner = z == owner_z(n)
    inner = jnp.logical_and(y > 0, y < NY - 1)

    barrier = pltpu.get_barrier_semaphore()

    def hello(device):
        pl.semaphore_signal(barrier, inc=1, device_id=device, device_id_type=MESH)

    @pl.when(is_owner)
    def _():
        @pl.loop(0, NZ)
        def _(i):
            v = lax.rem(z + NZ // 2 + i, NZ)
            for c in range(NN):
                @pl.when(jnp.logical_or(v != z, c != n))
                def _(c=c):
                    hello((base + v, c))

        for d in range(1, NY):
            hello((lax.rem(y + d, NY) * NZ + z, n))

    @pl.when(jnp.logical_not(is_owner))
    def _():
        hello((base + owner_z(n), n))

    for d in range(1, NN):
        hello((w, lax.rem(n + d, NN)))
    hello((above, n))
    hello((below, n))

    load = pltpu.make_async_copy(res_hbm.at[0, 0], res, load_sem)
    load.start()
    pivot_at = pl.ds(pl.multiple_of(PIVOT_PIECE * jnp.minimum(n, 5), PIVOT_PIECE), PIVOT_PIECE)
    pivot_load = pltpu.make_async_copy(piv_hbm.at[0, pivot_at], pivot_rows, pivot_sem)
    pivot_load.start()

    def inv_load(i):
        at = pl.ds(pl.multiple_of(i * HALF, HALF), HALF)
        return pltpu.make_async_copy(inv_hbm.at[0, 0, at], inv.at[at], inv_sem.at[i])

    @pl.loop(0, NI // HALF)
    def _(i):
        inv_load(i).start()

    basis = basis_ref[0, 0]
    scal = scal_ref[0]
    stack[...] = jnp.zeros_like(stack)
    for c in range(3):
        stack[32 * c : 32 * c + PC] = basis.astype(f32)
    for c, term in enumerate(split3(scal)):
        stack[PC + c : PC + c + 1] = term.astype(f32)
    stack[27:28] = scal
    for i in range(NI // 128):
        ext[128 * i : 128 * i + 128] = stack[:, 128 * i : 128 * i + 128].T
    load.wait()
    wgt[...] = (ext[:, 27:28] * res[...].astype(f32)).astype(bf16)
    primal = nn(basis, wgt[...])

    pm = jnp.broadcast_to(pmap_ref[0].astype(f32), (PC, PC))
    map_col = jnp.sum(jnp.where(iota((PC, PC), 0) == iota((PC, PC), 1), pm, 0.0), axis=1, keepdims=True)
    lane = iota((8, 128), 1)
    map_tile = jnp.zeros((8, 128), f32)
    for a in range(3):
        map_tile = jnp.where(lane == 96 + a, map_col[8 * a : 8 * a + 8], map_tile)
    for half in range(2):
        for m in range(4):
            tile = map_tile
            for a in range(3):
                piece = primal[8 * a : 8 * a + 8, 128 * half : 128 * half + 128]
                shift = 32 * ((a - m) % 4)
                if shift:
                    piece = pltpu.roll(piece, shift, 1)
                tile = jnp.where(lane // 32 == a, piece, tile)
            tiles[4 * half + m] = tile

    pl.semaphore_wait(barrier, (NN - 1) + 2 + NN + 9 * is_owner.astype(jnp.int32))

    def owned(c):
        return jnp.logical_and(is_owner, c == n)

    def turn(i):
        return lax.rem(i + n + z, NN)

    def deliver(src, dst, send, recv, device, here):
        @pl.when(here)
        def _():
            pltpu.make_async_copy(src, dst, recv).start()

        @pl.when(jnp.logical_not(here))
        def _():
            pltpu.make_async_remote_copy(
                src_ref=src, dst_ref=dst, send_sem=send, recv_sem=recv, device_id=device, device_id_type=MESH
            ).start()

    def sent(src, dst, send, recv, device, here):
        @pl.when(jnp.logical_not(here))
        def _():
            pltpu.make_async_remote_copy(
                src_ref=src, dst_ref=dst, send_sem=send, recv_sem=recv, device_id=device, device_id_type=MESH
            ).wait_send()

    piece_at = pl.ds(pl.multiple_of(n * PIECE, 8), PIECE)

    def prim_args(c):
        return (tiles.at[c], prim_in.at[z * NN + n], prim_send.at[c], prim_recv, (base + owner_z(c), c), owned(c))

    def sub_args(c):
        return (sub_hbm.at[0, piece_at], sub.at[z, piece_at], sub_send.at[c], sub_recv.at[z], (base + owner_z(c), c), owned(c))

    def piv_args(c):
        return (pivot_out, piv.at[z, pivot_at], piv_send.at[c], piv_recv, (base + owner_z(c), c), owned(c))

    def map_copy(c):
        return pltpu.make_async_remote_copy(
            src_ref=tiles.at[0], dst_ref=maps.at[n], send_sem=map_send.at[c], recv_sem=map_recv.at[n],
            device_id=(w, c), device_id_type=MESH,
        )

    def in_map(c):
        return pltpu.make_async_copy(maps.at[c], maps.at[c], map_recv.at[c])

    @pl.loop(0, NN)
    def _(i):
        deliver(*prim_args(turn(i)))

    @pl.loop(0, NN)
    def _(i):
        deliver(*sub_args(turn(i)))

    @pl.loop(0, NN)
    def _(i):
        c = turn(i)

        @pl.when(c != n)
        def _():
            map_copy(c).start()

    maps[n] = tiles[0]

    own_ext[...] = ext[...].astype(bf16)
    rows[:, 256:384] = jnp.where(iota((NI, 128), 1) < 32, ext[...], 0.0).astype(bf16)

    @pl.loop(0, NI // HALF)
    def _(i):
        at = pl.ds(pl.multiple_of(i * HALF, HALF), HALF)
        inv_load(i).wait()
        part = nn(inv[at], wgt[...])
        local[at] = part
        rows[at, 0:256] = part.astype(bf16)

    slot_lane = iota((1, TILE), 1)
    for k in range(NS):
        idxm[k : k + 1] = jnp.where(slot_lane < slen_ref[0, 0, k], sidx_ref[0, k], -1)

    @pl.loop(0, NI // TILE)
    def _(i):
        at = pl.ds(pl.multiple_of(i * TILE, TILE), TILE)
        row_id = iota((TILE, TILE), 0) + i * TILE
        for k in range(NS):
            select[at, TILE * k : TILE * k + TILE] = jnp.where(idxm[k : k + 1] == row_id, 1.0, 0.0).astype(bf16)

    pivot_load.wait()
    pivot_out[...] = pivot_rows[...].astype(bf16)

    @pl.when(n < G // PIVOT_PIECE)
    def _():
        @pl.loop(0, NN)
        def _(i):
            deliver(*piv_args(turn(i)))

    def pick_copy(k):
        to_w = jnp.where(k == 8, below, jnp.where(k == 9, above, w))
        to_n = jnp.where(k < 8, k, n)
        slot = jnp.where(k == 8, 9, jnp.where(k == 9, 8, n))
        return pltpu.make_async_remote_copy(
            src_ref=pick_out.at[k], dst_ref=pick_in.at[slot], send_sem=pick_send.at[k], recv_sem=pick_recv.at[slot],
            device_id=(to_w, to_n), device_id_type=MESH,
        )

    def in_pick(k):
        return pltpu.make_async_copy(pick_in.at[k], pick_in.at[k], pick_recv.at[k])

    def slot_at(i):
        return jnp.where(i < NN - 1, lax.rem(n + i + 1, NN), i + 1)

    def pick(i):
        k = slot_at(i)
        row = jnp.broadcast_to(idxm[pl.ds(k, 1)].astype(f32), (TILE, TILE))
        col = jnp.sum(jnp.where(iota((TILE, TILE), 0) == iota((TILE, TILE), 1), row, 0.0), axis=1, keepdims=True)
        hot = jnp.where(col.astype(jnp.int32) == iota((TILE, NI), 1), 1.0, 0.0).astype(bf16)
        picked = nn(hot, rows[...])
        pick_out[k, 0:TILE] = picked[:, 0:256].astype(bf16)
        for g in range(2):
            packed = picked[PACK * 4 * g : PACK * 4 * g + PACK, 256:384]
            for q in range(1, 4):
                at = PACK * (4 * g + q)
                packed = packed + pltpu.roll(picked[at : at + PACK, 256:384], 32 * q, 1)
            pick_out[k, TILE : TILE + PACK, 128 * g : 128 * g + 128] = packed.astype(bf16)

    pl.loop(0, jnp.where(is_owner, EARLY, NS - 1))(pick)

    def send_picks(first, last):
        @pl.loop(first, last)
        def _(i):
            pick_copy(slot_at(i)).start()

    @pl.when(jnp.logical_not(is_owner))
    def _():
        pl.semaphore_wait(go_sem, 1)
        send_picks(0, NS - 1)

    def y_copies(d):
        device = (lax.rem(y + d, NY) * NZ + z, n)
        parts = (
            (chain.at[NZ - 1, pl.ds(0, CH)], planes.at[y], y_send, y_recv),
            (product_out, products.at[y], t_send, t_recv),
        )
        return [
            pltpu.make_async_remote_copy(
                src_ref=src, dst_ref=dst, send_sem=send.at[d - 1], recv_sem=recv.at[y], device_id=device, device_id_type=MESH
            )
            for src, dst, send, recv in parts
        ]

    def back_copy(d):
        return pltpu.make_async_remote_copy(
            src_ref=xplanes.at[y], dst_ref=xplanes.at[y], send_sem=b_send.at[d - 1], recv_sem=b_recv.at[y],
            device_id=(lax.rem(y + d, NY) * NZ + z, n), device_id_type=MESH,
        )

    chunk_at = pl.ds(pl.multiple_of(n * CH, CH), CH)

    def x_args(v):
        return (x_out.at[v], xfull.at[chunk_at], x_send.at[v], x_recv, (base + v, n), v == z)

    @pl.when(is_owner)
    def _():
        pltpu.make_async_copy(prim_in, prim_in, prim_recv).wait()

        @pl.loop(0, NZ)
        def _(v):
            hots = []
            for c in range(NN):
                tile = prim_in[v * NN + c]
                for a in range(3):
                    at = PC * c + 8 * a
                    prim_v[at : at + 8] = pltpu.roll(tile, 128 - 32 * a, 1) if a else tile
                    col = tile[:, 96 + a : 97 + a].astype(jnp.int32)
                    hots.append(jnp.where(col == iota((8, G), 1), 1.0, 0.0))
            hot = jnp.concatenate(hots, axis=0).astype(bf16)
            high, middle, low = split3(prim_v[...].T[:CH])
            rhs[v] = nn(high, hot) + (nn(middle, hot) + nn(low, hot))

        def in_sub(v):
            pltpu.make_async_copy(sub.at[v], sub.at[v], sub_recv.at[v]).wait()

        for v in range(NZ):
            in_sub(v)

        @pl.loop(0, NZ)
        def _(v):
            @pl.when(v != z)
            def _():
                pl.semaphore_signal(go_sem, inc=1, device_id=(base + v, n), device_id_type=MESH)

        eye = jnp.where(iota((G, G), 0) == iota((G, G), 1), 1.0, 0.0)
        chain[0, 0:CH] = rhs[0]
        first_high, first_low = split2(sub[0])
        chain[0, CH:CARRY] = -(nt(eye.astype(bf16), first_high) + nt(eye.astype(bf16), first_low))

        @pl.loop(1, NZ)
        def _(v):
            step = dot3(nt, chain[v - 1], sub[v])
            chain[v, 0:CH] = rhs[v] - step[0:CH]
            chain[v, CH:CARRY] = -step[CH:CARRY]

        product_out[...] = chain[NZ - 1, CH:CARRY].astype(bf16)
        for d in range(1, NY):
            y_copies(d)[0].start()

        @pl.when(inner)
        def _():
            for d in range(1, NY):
                y_copies(d)[1].start()

        planes[y] = chain[NZ - 1, 0:CH]

        send_picks(0, EARLY)

    pl.loop(jnp.where(is_owner, EARLY, NS - 1), NS - 1)(pick)

    @pl.when(is_owner)
    def _():
        send_picks(EARLY, NS - 1)
        high_carry[NZ - 1] = -jnp.where(iota((G, G), 0) == iota((G, G), 1), 1.0, 0.0)

        @pl.loop(0, NZ - 1)
        def _(i):
            v = NZ - 2 - i
            high_carry[v] = -dot3(nn, high_carry[v + 1], sub[v + 1])

        pltpu.make_async_copy(piv, piv, piv_recv).wait()

    @pl.when(is_owner)
    def _():
        def in_plane(d):
            src = lax.rem(y + NY - d, NY)
            values = planes.at[src]
            pltpu.make_async_copy(values, values, y_recv.at[src]).wait()

            @pl.when(jnp.logical_and(src > 0, src < NY - 1))
            def _():
                product = products.at[src]
                pltpu.make_async_copy(product, product, t_recv.at[src]).wait()


        for d in range(1, NY):
            in_plane(d)
        carry[...] = jnp.where(y > 0, planes[0], 0.0)
        for g in range(1, NY - 1):
            @pl.when(y > g)
            def _(g=g):
                high, low = split2(carry[...])
                carry[...] = planes[g] + (nn(high, products[g]) + nn(low, products[g]))

        for v in range(NZ):
            solved = chain[v, 0:CH] + dot3(nn, carry[...], chain[v, CH:CARRY])
            high, low = split2(solved)
            pivoted[v] = nn(high, piv[v]) + nn(low, piv[v])
        xs[NZ - 1] = pivoted[NZ - 1]

        @pl.loop(0, NZ - 1)
        def _(i):
            v = NZ - 2 - i
            xs[v] = pivoted[v] - dot3(nn, xs[v + 1], sub[v + 1])

        xplanes[y] = dot3(nn, xs[0], sub[0])
        for d in range(1, NY):
            back_copy(d).start()
        for d in range(1, NY):
            src = lax.rem(y + NY - d, NY)
            pltpu.make_async_copy(xplanes.at[src], xplanes.at[src], b_recv.at[src]).wait()
        carry[...] = jnp.where(y < NY - 1, xplanes[NY - 1], 0.0)
        for g in range(NY - 2, 0, -1):
            @pl.when(y < g)
            def _(g=g):
                high, low = split2(carry[...])
                carry[...] = xplanes[g] + (nt(high, products[g]) + nt(low, products[g]))

        for v in range(NZ):
            x_out[v] = (xs[v] + dot3(nn, carry[...], high_carry[v])).astype(bf16)

        @pl.loop(0, NZ)
        def _(v):
            deliver(*x_args(v))

    def gather_copy(c):
        return pltpu.make_async_remote_copy(
            src_ref=xfull.at[chunk_at], dst_ref=xfull.at[chunk_at], send_sem=gather_send.at[c], recv_sem=gather_recv.at[n],
            device_id=(w, c), device_id_type=MESH,
        )

    pltpu.make_async_copy(xfull.at[chunk_at], xfull.at[chunk_at], x_recv).wait()

    @pl.loop(1, NN)
    def _(d):
        gather_copy(lax.rem(n + d, NN)).start()

    @pl.loop(0, NN)
    def _(c):
        @pl.when(c != n)
        def _():
            in_map(c).wait()

    for c in range(NN):
        tile = maps[c]
        for a in range(3):
            col = tile[:, 96 + a : 97 + a].astype(jnp.int32)
            spread_map[32 * c + 8 * a : 32 * c + 8 * a + 8] = jnp.where(col == iota((8, G), 1), 1.0, 0.0)
        spread_map[32 * c + PC : 32 * c + 32] = jnp.zeros((32 - PC, G), f32)
    vals[:, 32:128] = jnp.zeros((NS, 96, R), bf16)

    @pl.loop(0, NS)
    def _(k):
        at = pl.ds(pl.multiple_of(k * TILE, TILE), TILE)

        @pl.when(k == n)
        def _():
            part_in[at] = jnp.zeros((TILE, R), f32)
            ext_in[at] = jnp.zeros((TILE, 128), bf16)
            weight_in[at] = jnp.zeros((TILE, 128), f32)

        @pl.when(k != n)
        def _():
            in_pick(k).wait()
            pieces = []
            packed = pick_in[k, TILE : TILE + PACK].astype(f32)
            for q in range(8):
                piece = packed[:, 128 * (q // 4) : 128 * (q // 4) + 128]
                pieces.append(pltpu.roll(piece, 128 - 32 * (q % 4), 1) if q % 4 else piece)
            extra = jnp.where(iota((TILE, 128), 1) < 32, jnp.concatenate(pieces, axis=0), 0.0)
            weight = extra[:, PC : PC + 1] + extra[:, PC + 1 : PC + 2] + extra[:, PC + 2 : PC + 3]
            ext_in[at] = (extra + (pltpu.roll(extra, 32, 1) + pltpu.roll(extra, 64, 1))).astype(bf16)
            weight_in[at] = jnp.broadcast_to(weight, (TILE, 128))
            part_in[at] = weight * pick_in[k, 0:TILE].astype(f32)

    @pl.loop(1, NN)
    def _(d):
        src = lax.rem(n + d, NN)
        at = pl.ds(pl.multiple_of(src * CH, CH), CH)
        pltpu.make_async_copy(xfull.at[at], xfull.at[at], gather_recv.at[src]).wait()

    hot = spread_map[...].astype(bf16)
    coarse_vals = nt(hot, xfull[...]).astype(bf16)
    for j in range(NN):
        vals[j, 0:32] = coarse_vals[32 * j : 32 * j + 32]

    def val_copy(side):
        return pltpu.make_async_remote_copy(
            src_ref=vals.at[n, pl.ds(0, 32)], dst_ref=vals.at[8 + side, pl.ds(0, 32)],
            send_sem=val_send.at[side], recv_sem=val_recv.at[side],
            device_id=(above if side == 0 else below, n), device_id_type=MESH,
        )

    for side in range(2):
        val_copy(side).start()

    def receive(k):
        at = slice(k * TILE, k * TILE + TILE)
        spread = nn(ext_in[at], vals[k])
        weight = weight_in[at]
        for half in (slice(0, 128), slice(128, 256)):
            inc[at, half] = (part_in[at, half] + weight * spread[:, half]).astype(bf16)

    for k in range(NN):
        receive(k)

    @pl.loop(0, NI // HALF)
    def _(i):
        at = pl.ds(pl.multiple_of(i * HALF, HALF), HALF)
        spread = nn(own_ext[at], vals[n])
        combined = (ext[at, 27:28] * (local[at] + spread)).astype(bf16)
        result[at] = combined.astype(f32) + nn(select[at, 0 : NN * TILE], inc[0 : NN * TILE])

    for side in range(2):
        into = vals.at[8 + side, pl.ds(0, 32)]
        pltpu.make_async_copy(into, into, val_recv.at[side]).wait()
        receive(8 + side)

    def store(i):
        at = pl.ds(pl.multiple_of(i * HALF, HALF), HALF)
        return pltpu.make_async_copy(result.at[at], out_hbm.at[0, 0, at], out_sem.at[i])

    @pl.loop(0, NI // HALF)
    def _(i):
        at = pl.ds(pl.multiple_of(i * HALF, HALF), HALF)
        result[at] += nn(select[at, NN * TILE : NS * TILE], inc[NN * TILE : NS * TILE])
        store(i).start()

    @pl.loop(0, NN)
    def _(c):
        sent(*prim_args(c))
        sent(*sub_args(c))

        @pl.when(n < G // PIVOT_PIECE)
        def _():
            sent(*piv_args(c))

        @pl.when(c != n)
        def _():
            map_copy(c).wait_send()
            gather_copy(c).wait_send()

    @pl.loop(0, NS)
    def _(k):
        @pl.when(k != n)
        def _():
            pick_copy(k).wait_send()

    for side in range(2):
        val_copy(side).wait_send()

    @pl.when(is_owner)
    def _():
        for d in range(1, NY):
            y_copies(d)[0].wait_send()
            back_copy(d).wait_send()

        @pl.when(inner)
        def _():
            for d in range(1, NY):
                y_copies(d)[1].wait_send()

        @pl.loop(0, NZ)
        def _(v):
            sent(*x_args(v))

    @pl.loop(0, NI // HALF)
    def _(i):
        store(i).wait()


def body(residual, scaling, inverse, basis, primal_map, slot_index, slot_length, sub, pivot):
    vmem = pl.BlockSpec(memory_space=pltpu.VMEM)
    smem = pl.BlockSpec(memory_space=pltpu.SMEM)
    hbm = pl.BlockSpec(memory_space=pl.ANY)
    dma = pltpu.SemaphoreType.DMA
    V = pltpu.VMEM
    return pl.pallas_call(
        kernel,
        out_shape=jax.ShapeDtypeStruct((1, 1, NI, R), f32),
        in_specs=[hbm, vmem, hbm, vmem, vmem, vmem, smem, hbm, hbm],
        out_specs=hbm,
        scratch_shapes=[
            V((NI, R), bf16), V((NI, NI), bf16), V((NI, R), bf16), V((NI, R), f32), V((NI, 384), bf16), V((NI, 128), f32),
            V((NI, NS * TILE), bf16), V((NS, TILE + PACK, 256), bf16), V((NS, TILE + PACK, 256), bf16), V((NS * TILE, R), bf16),
            V((NI, R), f32), V((NS * TILE, R), f32), V((NS * TILE, 128), bf16), V((NS * TILE, 128), f32), V((NI, 128), bf16),
            V((PIVOT_PIECE, G), f32), V((PIVOT_PIECE, G), bf16),
            V((16, TILE), jnp.int32), V((NN, 8, 128), f32), V((NN, 8, 128), f32), V((NN * 32, G), f32), V((NS, 128, R), bf16),
            V((R, G), bf16), V((128, NI), f32),
            V((NZ * NN, 8, 128), f32), V((G, 128), f32), V((NZ, G, G), f32), V((NZ, G, G), bf16), V((NZ, CARRY, G), f32),
            V((NZ, CH, G), f32), V((NY, CH, G), f32), V((NZ, G, G), f32), V((NZ, CH, G), f32), V((NZ, CH, G), f32),
            V((NY, CH, G), f32), V((CH, G), f32), V((NZ, CH, G), bf16), V((G, G), bf16), V((NY, G, G), bf16),
            dma, dma, dma((NI // HALF,)), dma((NI // HALF,)),
            dma((NN,)), dma, dma((NN,)), dma((NZ,)), dma((NN,)), dma,
            dma((NN,)), dma((NN,)), dma((NS,)), dma((NS,)),
            dma((NY - 1,)), dma((NY,)), dma((NY - 1,)), dma((NY,)), dma((NY - 1,)), dma((NY,)),
            dma((NZ,)), dma, dma((NN,)), dma((NN,)), dma((2,)), dma((2,)), pltpu.SemaphoreType.REGULAR,
        ],
        compiler_params=pltpu.CompilerParams(collective_id=0, has_side_effects=True, vmem_limit_bytes=58 * 2**20),
    )(residual, scaling, inverse, basis, primal_map, slot_index.transpose(0, 2, 1, 3), slot_length, sub, pivot)


def solution(mesh):
    in_specs = (
        P("wide", "narrow", None, None),
        P("wide", "narrow", None),
        P("wide", "narrow", None, None),
        P("wide", "narrow", None, None),
        P("wide", "narrow", None),
        P("wide", "narrow", None, None),
        P("wide", "narrow", None),
        P("wide", None, None),
        P("wide", None, None),
    )
    out_specs = P("wide", "narrow", None, None)
    return jax.shard_map(body, mesh=mesh, in_specs=in_specs, out_specs=out_specs, check_vma=False)
```

```python
import jax
import jax.numpy as jnp
from jax import lax
from jax.experimental import pallas as pl
from jax.experimental.pallas import tpu as pltpu
from jax.sharding import PartitionSpec as P

MESH = pl.DeviceIdType.MESH
f32 = jnp.float32
bf16 = jnp.bfloat16
NZ = 8
NY = 4
NN = 8
NS = 10
NI = 2048
R = 256
PC = 24
G = 192
CH = R // NN
PIECE = G // NN
PIVOT_PIECE = 32
CARRY = CH + G
TILE = 256
HALF = 512
PACK = TILE // 8
EARLY = 4


def owner_z(n):
    return n // 2 + 4 * (n % 2)


def iota(shape, axis):
    return lax.broadcasted_iota(jnp.int32, shape, axis)


def split2(a):
    high = a.astype(bf16)
    return high, (a - high.astype(f32)).astype(bf16)


def split3(a):
    high = a.astype(bf16)
    rest = a - high.astype(f32)
    middle = rest.astype(bf16)
    return high, middle, (rest - middle.astype(f32)).astype(bf16)


def nn(a, b):
    return lax.dot_general(a, b, (((1,), (0,)), ((), ())), preferred_element_type=f32)


def nt(a, b):
    return lax.dot_general(a, b, (((1,), (1,)), ((), ())), preferred_element_type=f32)


def dot3(dot, a, b):
    a_high, a_low = split2(a)
    b_high, b_low = split2(b)
    return dot(a_high, b_high) + (dot(a_high, b_low) + dot(a_low, b_high))


def kernel(
    res_hbm, scal_ref, inv_hbm, basis_ref, pmap_ref, sidx_ref, slen_ref, sub_hbm, piv_hbm,
    out_hbm,
    res, inv, wgt, local, rows, ext, select, pick_out, pick_in, inc, result,
    part_in, ext_in, weight_in, own_ext, pivot_rows, pivot_out,
    idxm, tiles, maps, spread_map, vals, xfull, stack,
    prim_in, prim_v, sub, piv, chain, rhs, planes, high_carry, pivoted, xs, xplanes, carry, product_out, products,
    load_sem, pivot_sem, inv_sem, out_sem,
    prim_send, prim_recv, sub_send, sub_recv, piv_send, piv_recv,
    map_send, map_recv, pick_send, pick_recv,
    y_send, y_recv, t_send, t_recv, b_send, b_recv,
    x_send, x_recv, gather_send, gather_recv, val_send, val_recv, go_sem,
):
    w = lax.axis_index("wide")
    n = lax.axis_index("narrow")
    y = w // NZ
    z = w % NZ
    base = y * NZ
    above = lax.rem(w + 1, NY * NZ)
    below = lax.rem(w + NY * NZ - 1, NY * NZ)
    is_owner = z == owner_z(n)
    inner = jnp.logical_and(y > 0, y < NY - 1)

    barrier = pltpu.get_barrier_semaphore()

    def hello(device):
        pl.semaphore_signal(barrier, inc=1, device_id=device, device_id_type=MESH)

    @pl.when(is_owner)
    def _():
        @pl.loop(0, NZ)
        def _(i):
            v = lax.rem(z + NZ // 2 + i, NZ)
            for c in range(NN):
                @pl.when(jnp.logical_or(v != z, c != n))
                def _(c=c):
                    hello((base + v, c))

        for d in range(1, NY):
            hello((lax.rem(y + d, NY) * NZ + z, n))

    @pl.when(jnp.logical_not(is_owner))
    def _():
        hello((base + owner_z(n), n))

    for d in range(1, NN):
        hello((w, lax.rem(n + d, NN)))
    hello((above, n))
    hello((below, n))

    load = pltpu.make_async_copy(res_hbm.at[0, 0], res, load_sem)
    load.start()
    pivot_at = pl.ds(pl.multiple_of(PIVOT_PIECE * jnp.minimum(n, 5), PIVOT_PIECE), PIVOT_PIECE)
    pivot_load = pltpu.make_async_copy(piv_hbm.at[0, pivot_at], pivot_rows, pivot_sem)
    pivot_load.start()

    def inv_load(i):
        at = pl.ds(pl.multiple_of(i * HALF, HALF), HALF)
        return pltpu.make_async_copy(inv_hbm.at[0, 0, at], inv.at[at], inv_sem.at[i])

    @pl.loop(0, NI // HALF)
    def _(i):
        inv_load(i).start()

    basis = basis_ref[0, 0]
    scal = scal_ref[0]
    stack[...] = jnp.zeros_like(stack)
    for c in range(3):
        stack[32 * c : 32 * c + PC] = basis.astype(f32)
    for c, term in enumerate(split3(scal)):
        stack[PC + c : PC + c + 1] = term.astype(f32)
    stack[27:28] = scal
    for i in range(NI // 128):
        ext[128 * i : 128 * i + 128] = stack[:, 128 * i : 128 * i + 128].T
    load.wait()
    wgt[...] = (ext[:, 27:28] * res[...].astype(f32)).astype(bf16)
    primal = nn(basis, wgt[...])

    pm = jnp.broadcast_to(pmap_ref[0].astype(f32), (PC, PC))
    map_col = jnp.sum(jnp.where(iota((PC, PC), 0) == iota((PC, PC), 1), pm, 0.0), axis=1, keepdims=True)
    lane = iota((8, 128), 1)
    map_tile = jnp.zeros((8, 128), f32)
    for a in range(3):
        map_tile = jnp.where(lane == 96 + a, map_col[8 * a : 8 * a + 8], map_tile)
    for half in range(2):
        for m in range(4):
            tile = map_tile
            for a in range(3):
                piece = primal[8 * a : 8 * a + 8, 128 * half : 128 * half + 128]
                shift = 32 * ((a - m) % 4)
                if shift:
                    piece = pltpu.roll(piece, shift, 1)
                tile = jnp.where(lane // 32 == a, piece, tile)
            tiles[4 * half + m] = tile

    pl.semaphore_wait(barrier, (NN - 1) + 2 + NN + 9 * is_owner.astype(jnp.int32))

    def owned(c):
        return jnp.logical_and(is_owner, c == n)

    def turn(i):
        return lax.rem(i + n + z, NN)

    def deliver(src, dst, send, recv, device, here):
        @pl.when(here)
        def _():
            pltpu.make_async_copy(src, dst, recv).start()

        @pl.when(jnp.logical_not(here))
        def _():
            pltpu.make_async_remote_copy(
                src_ref=src, dst_ref=dst, send_sem=send, recv_sem=recv, device_id=device, device_id_type=MESH
            ).start()

    def sent(src, dst, send, recv, device, here):
        @pl.when(jnp.logical_not(here))
        def _():
            pltpu.make_async_remote_copy(
                src_ref=src, dst_ref=dst, send_sem=send, recv_sem=recv, device_id=device, device_id_type=MESH
            ).wait_send()

    piece_at = pl.ds(pl.multiple_of(n * PIECE, 8), PIECE)

    def prim_args(c):
        return (tiles.at[c], prim_in.at[z * NN + n], prim_send.at[c], prim_recv, (base + owner_z(c), c), owned(c))

    def sub_args(c):
        return (sub_hbm.at[0, piece_at], sub.at[z, piece_at], sub_send.at[c], sub_recv.at[z], (base + owner_z(c), c), owned(c))

    def piv_args(c):
        return (pivot_out, piv.at[z, pivot_at], piv_send.at[c], piv_recv, (base + owner_z(c), c), owned(c))

    def map_copy(c):
        return pltpu.make_async_remote_copy(
            src_ref=tiles.at[0], dst_ref=maps.at[n], send_sem=map_send.at[c], recv_sem=map_recv.at[n],
            device_id=(w, c), device_id_type=MESH,
        )

    def in_map(c):
        return pltpu.make_async_copy(maps.at[c], maps.at[c], map_recv.at[c])

    @pl.loop(0, NN)
    def _(i):
        deliver(*prim_args(turn(i)))

    @pl.loop(0, NN)
    def _(i):
        deliver(*sub_args(turn(i)))

    @pl.loop(0, NN)
    def _(i):
        c = turn(i)

        @pl.when(c != n)
        def _():
            map_copy(c).start()

    maps[n] = tiles[0]

    own_ext[...] = ext[...].astype(bf16)
    rows[:, 256:384] = jnp.where(iota((NI, 128), 1) < 32, ext[...], 0.0).astype(bf16)

    @pl.loop(0, NI // HALF)
    def _(i):
        at = pl.ds(pl.multiple_of(i * HALF, HALF), HALF)
        inv_load(i).wait()
        part = nn(inv[at], wgt[...])
        local[at] = part
        rows[at, 0:256] = part.astype(bf16)

    slot_lane = iota((1, TILE), 1)
    for k in range(NS):
        idxm[k : k + 1] = jnp.where(slot_lane < slen_ref[0, 0, k], sidx_ref[0, k], -1)

    @pl.loop(0, NI // TILE)
    def _(i):
        at = pl.ds(pl.multiple_of(i * TILE, TILE), TILE)
        row_id = iota((TILE, TILE), 0) + i * TILE
        for k in range(NS):
            select[at, TILE * k : TILE * k + TILE] = jnp.where(idxm[k : k + 1] == row_id, 1.0, 0.0).astype(bf16)

    pivot_load.wait()
    pivot_out[...] = pivot_rows[...].astype(bf16)

    @pl.when(n < G // PIVOT_PIECE)
    def _():
        @pl.loop(0, NN)
        def _(i):
            deliver(*piv_args(turn(i)))

    def pick_copy(k):
        to_w = jnp.where(k == 8, below, jnp.where(k == 9, above, w))
        to_n = jnp.where(k < 8, k, n)
        slot = jnp.where(k == 8, 9, jnp.where(k == 9, 8, n))
        return pltpu.make_async_remote_copy(
            src_ref=pick_out.at[k], dst_ref=pick_in.at[slot], send_sem=pick_send.at[k], recv_sem=pick_recv.at[slot],
            device_id=(to_w, to_n), device_id_type=MESH,
        )

    def in_pick(k):
        return pltpu.make_async_copy(pick_in.at[k], pick_in.at[k], pick_recv.at[k])

    def slot_at(i):
        return jnp.where(i < NN - 1, lax.rem(n + i + 1, NN), i + 1)

    def pick(i):
        k = slot_at(i)
        row = jnp.broadcast_to(idxm[pl.ds(k, 1)].astype(f32), (TILE, TILE))
        col = jnp.sum(jnp.where(iota((TILE, TILE), 0) == iota((TILE, TILE), 1), row, 0.0), axis=1, keepdims=True)
        hot = jnp.where(col.astype(jnp.int32) == iota((TILE, NI), 1), 1.0, 0.0).astype(bf16)
        picked = nn(hot, rows[...])
        pick_out[k, 0:TILE] = picked[:, 0:256].astype(bf16)
        for g in range(2):
            packed = picked[PACK * 4 * g : PACK * 4 * g + PACK, 256:384]
            for q in range(1, 4):
                at = PACK * (4 * g + q)
                packed = packed + pltpu.roll(picked[at : at + PACK, 256:384], 32 * q, 1)
            pick_out[k, TILE : TILE + PACK, 128 * g : 128 * g + 128] = packed.astype(bf16)

    pl.loop(0, jnp.where(is_owner, EARLY, NS - 1))(pick)

    def send_picks(first, last):
        @pl.loop(first, last)
        def _(i):
            pick_copy(slot_at(i)).start()

    @pl.when(jnp.logical_not(is_owner))
    def _():
        pl.semaphore_wait(go_sem, 1)
        send_picks(0, NS - 1)

    def y_copies(d):
        device = (lax.rem(y + d, NY) * NZ + z, n)
        parts = (
            (chain.at[NZ - 1, pl.ds(0, CH)], planes.at[y], y_send, y_recv),
            (product_out, products.at[y], t_send, t_recv),
        )
        return [
            pltpu.make_async_remote_copy(
                src_ref=src, dst_ref=dst, send_sem=send.at[d - 1], recv_sem=recv.at[y], device_id=device, device_id_type=MESH
            )
            for src, dst, send, recv in parts
        ]

    def back_copy(d):
        return pltpu.make_async_remote_copy(
            src_ref=xplanes.at[y], dst_ref=xplanes.at[y], send_sem=b_send.at[d - 1], recv_sem=b_recv.at[y],
            device_id=(lax.rem(y + d, NY) * NZ + z, n), device_id_type=MESH,
        )

    chunk_at = pl.ds(pl.multiple_of(n * CH, CH), CH)

    def x_args(v):
        return (xs.at[v], xfull.at[chunk_at], x_send.at[v], x_recv, (base + v, n), v == z)

    @pl.when(is_owner)
    def _():
        pltpu.make_async_copy(prim_in, prim_in, prim_recv).wait()

        @pl.loop(0, NZ)
        def _(v):
            hots = []
            for c in range(NN):
                tile = prim_in[v * NN + c]
                for a in range(3):
                    at = PC * c + 8 * a
                    prim_v[at : at + 8] = pltpu.roll(tile, 128 - 32 * a, 1) if a else tile
                    col = tile[:, 96 + a : 97 + a].astype(jnp.int32)
                    hots.append(jnp.where(col == iota((8, G), 1), 1.0, 0.0))
            hot = jnp.concatenate(hots, axis=0).astype(bf16)
            high, middle, low = split3(prim_v[...].T[:CH])
            rhs[v] = nn(high, hot) + (nn(middle, hot) + nn(low, hot))

        def in_sub(v):
            pltpu.make_async_copy(sub.at[v], sub.at[v], sub_recv.at[v]).wait()

        for v in range(NZ):
            in_sub(v)

        @pl.loop(0, NZ)
        def _(v):
            @pl.when(v != z)
            def _():
                pl.semaphore_signal(go_sem, inc=1, device_id=(base + v, n), device_id_type=MESH)

        eye = jnp.where(iota((G, G), 0) == iota((G, G), 1), 1.0, 0.0)
        chain[0, 0:CH] = rhs[0]
        first_high, first_low = split2(sub[0])
        chain[0, CH:CARRY] = -(nt(eye.astype(bf16), first_high) + nt(eye.astype(bf16), first_low))

        @pl.loop(1, NZ)
        def _(v):
            step = dot3(nt, chain[v - 1], sub[v])
            chain[v, 0:CH] = rhs[v] - step[0:CH]
            chain[v, CH:CARRY] = -step[CH:CARRY]

        product_out[...] = chain[NZ - 1, CH:CARRY].astype(bf16)
        for d in range(1, NY):
            y_copies(d)[0].start()

        @pl.when(inner)
        def _():
            for d in range(1, NY):
                y_copies(d)[1].start()

        planes[y] = chain[NZ - 1, 0:CH]

        send_picks(0, EARLY)

    pl.loop(jnp.where(is_owner, EARLY, NS - 1), NS - 1)(pick)

    @pl.when(is_owner)
    def _():
        send_picks(EARLY, NS - 1)
        high_carry[NZ - 1] = -jnp.where(iota((G, G), 0) == iota((G, G), 1), 1.0, 0.0)

        @pl.loop(0, NZ - 1)
        def _(i):
            v = NZ - 2 - i
            high_carry[v] = -dot3(nn, high_carry[v + 1], sub[v + 1])

        pltpu.make_async_copy(piv, piv, piv_recv).wait()

    @pl.when(is_owner)
    def _():
        def in_plane(d):
            src = lax.rem(y + NY - d, NY)
            values = planes.at[src]
            pltpu.make_async_copy(values, values, y_recv.at[src]).wait()

            @pl.when(jnp.logical_and(src > 0, src < NY - 1))
            def _():
                product = products.at[src]
                pltpu.make_async_copy(product, product, t_recv.at[src]).wait()


        for d in range(1, NY):
            in_plane(d)
        carry[...] = jnp.where(y > 0, planes[0], 0.0)
        for g in range(1, NY - 1):
            @pl.when(y > g)
            def _(g=g):
                high, low = split2(carry[...])
                carry[...] = planes[g] + (nn(high, products[g]) + nn(low, products[g]))

        for v in range(NZ):
            solved = chain[v, 0:CH] + dot3(nn, carry[...], chain[v, CH:CARRY])
            high, low = split2(solved)
            pivoted[v] = nn(high, piv[v]) + nn(low, piv[v])
        xs[NZ - 1] = pivoted[NZ - 1]

        @pl.loop(0, NZ - 1)
        def _(i):
            v = NZ - 2 - i
            xs[v] = pivoted[v] - dot3(nn, xs[v + 1], sub[v + 1])

        xplanes[y] = dot3(nn, xs[0], sub[0])
        for d in range(1, NY):
            back_copy(d).start()
        for d in range(1, NY):
            src = lax.rem(y + NY - d, NY)
            pltpu.make_async_copy(xplanes.at[src], xplanes.at[src], b_recv.at[src]).wait()
        carry[...] = jnp.where(y < NY - 1, xplanes[NY - 1], 0.0)
        for g in range(NY - 2, 0, -1):
            @pl.when(y < g)
            def _(g=g):
                high, low = split2(carry[...])
                carry[...] = xplanes[g] + (nt(high, products[g]) + nt(low, products[g]))

        for v in range(NZ):
            xs[v] = xs[v] + dot3(nn, carry[...], high_carry[v])

        @pl.loop(0, NZ)
        def _(v):
            deliver(*x_args(v))

    def gather_copy(c):
        return pltpu.make_async_remote_copy(
            src_ref=xfull.at[chunk_at], dst_ref=xfull.at[chunk_at], send_sem=gather_send.at[c], recv_sem=gather_recv.at[n],
            device_id=(w, c), device_id_type=MESH,
        )

    pltpu.make_async_copy(xfull.at[chunk_at], xfull.at[chunk_at], x_recv).wait()

    @pl.loop(1, NN)
    def _(d):
        gather_copy(lax.rem(n + d, NN)).start()

    @pl.loop(0, NN)
    def _(c):
        @pl.when(c != n)
        def _():
            in_map(c).wait()

    for c in range(NN):
        tile = maps[c]
        for a in range(3):
            col = tile[:, 96 + a : 97 + a].astype(jnp.int32)
            spread_map[32 * c + 8 * a : 32 * c + 8 * a + 8] = jnp.where(col == iota((8, G), 1), 1.0, 0.0)
        spread_map[32 * c + PC : 32 * c + 32] = jnp.zeros((32 - PC, G), f32)
    vals[:, 96:128] = jnp.zeros((NS, 32, R), bf16)

    @pl.loop(0, NS)
    def _(k):
        at = pl.ds(pl.multiple_of(k * TILE, TILE), TILE)

        @pl.when(k == n)
        def _():
            part_in[at] = jnp.zeros((TILE, R), f32)
            ext_in[at] = jnp.zeros((TILE, 128), bf16)
            weight_in[at] = jnp.zeros((TILE, 128), f32)

        @pl.when(k != n)
        def _():
            in_pick(k).wait()
            pieces = []
            packed = pick_in[k, TILE : TILE + PACK].astype(f32)
            for q in range(8):
                piece = packed[:, 128 * (q // 4) : 128 * (q // 4) + 128]
                pieces.append(pltpu.roll(piece, 128 - 32 * (q % 4), 1) if q % 4 else piece)
            extra = jnp.where(iota((TILE, 128), 1) < 32, jnp.concatenate(pieces, axis=0), 0.0)
            weight = extra[:, PC : PC + 1] + extra[:, PC + 1 : PC + 2] + extra[:, PC + 2 : PC + 3]
            ext_in[at] = (extra + (pltpu.roll(extra, 32, 1) + pltpu.roll(extra, 64, 1))).astype(bf16)
            weight_in[at] = jnp.broadcast_to(weight, (TILE, 128))
            part_in[at] = weight * pick_in[k, 0:TILE].astype(f32)

    @pl.loop(1, NN)
    def _(d):
        src = lax.rem(n + d, NN)
        at = pl.ds(pl.multiple_of(src * CH, CH), CH)
        pltpu.make_async_copy(xfull.at[at], xfull.at[at], gather_recv.at[src]).wait()

    hot = spread_map[...].astype(bf16)
    for c, term in enumerate(split3(xfull[...])):
        picked = nt(hot, term).astype(bf16)
        for j in range(NN):
            vals[j, 32 * c : 32 * c + 32] = picked[32 * j : 32 * j + 32]

    def val_copy(side):
        return pltpu.make_async_remote_copy(
            src_ref=vals.at[n, pl.ds(0, 96)], dst_ref=vals.at[8 + side, pl.ds(0, 96)],
            send_sem=val_send.at[side], recv_sem=val_recv.at[side],
            device_id=(above if side == 0 else below, n), device_id_type=MESH,
        )

    for side in range(2):
        val_copy(side).start()

    def receive(k):
        at = slice(k * TILE, k * TILE + TILE)
        spread = nn(ext_in[at], vals[k])
        weight = weight_in[at]
        for half in (slice(0, 128), slice(128, 256)):
            inc[at, half] = (part_in[at, half] + weight * spread[:, half]).astype(bf16)

    for k in range(NN):
        receive(k)

    @pl.loop(0, NI // HALF)
    def _(i):
        at = pl.ds(pl.multiple_of(i * HALF, HALF), HALF)
        spread = nn(own_ext[at], vals[n])
        combined = (ext[at, 27:28] * (local[at] + spread)).astype(bf16)
        result[at] = combined.astype(f32) + nn(select[at, 0 : NN * TILE], inc[0 : NN * TILE])

    for side in range(2):
        into = vals.at[8 + side, pl.ds(0, 96)]
        pltpu.make_async_copy(into, into, val_recv.at[side]).wait()
        receive(8 + side)

    def store(i):
        at = pl.ds(pl.multiple_of(i * HALF, HALF), HALF)
        return pltpu.make_async_copy(result.at[at], out_hbm.at[0, 0, at], out_sem.at[i])

    @pl.loop(0, NI // HALF)
    def _(i):
        at = pl.ds(pl.multiple_of(i * HALF, HALF), HALF)
        result[at] += nn(select[at, NN * TILE : NS * TILE], inc[NN * TILE : NS * TILE])
        store(i).start()

    @pl.loop(0, NN)
    def _(c):
        sent(*prim_args(c))
        sent(*sub_args(c))

        @pl.when(n < G // PIVOT_PIECE)
        def _():
            sent(*piv_args(c))

        @pl.when(c != n)
        def _():
            map_copy(c).wait_send()
            gather_copy(c).wait_send()

    @pl.loop(0, NS)
    def _(k):
        @pl.when(k != n)
        def _():
            pick_copy(k).wait_send()

    for side in range(2):
        val_copy(side).wait_send()

    @pl.when(is_owner)
    def _():
        for d in range(1, NY):
            y_copies(d)[0].wait_send()
            back_copy(d).wait_send()

        @pl.when(inner)
        def _():
            for d in range(1, NY):
                y_copies(d)[1].wait_send()

        @pl.loop(0, NZ)
        def _(v):
            sent(*x_args(v))

    @pl.loop(0, NI // HALF)
    def _(i):
        store(i).wait()


def body(residual, scaling, inverse, basis, primal_map, slot_index, slot_length, sub, pivot):
    vmem = pl.BlockSpec(memory_space=pltpu.VMEM)
    smem = pl.BlockSpec(memory_space=pltpu.SMEM)
    hbm = pl.BlockSpec(memory_space=pl.ANY)
    dma = pltpu.SemaphoreType.DMA
    V = pltpu.VMEM
    return pl.pallas_call(
        kernel,
        out_shape=jax.ShapeDtypeStruct((1, 1, NI, R), f32),
        in_specs=[hbm, vmem, hbm, vmem, vmem, vmem, smem, hbm, hbm],
        out_specs=hbm,
        scratch_shapes=[
            V((NI, R), bf16), V((NI, NI), bf16), V((NI, R), bf16), V((NI, R), f32), V((NI, 384), bf16), V((NI, 128), f32),
            V((NI, NS * TILE), bf16), V((NS, TILE + PACK, 256), bf16), V((NS, TILE + PACK, 256), bf16), V((NS * TILE, R), bf16),
            V((NI, R), f32), V((NS * TILE, R), f32), V((NS * TILE, 128), bf16), V((NS * TILE, 128), f32), V((NI, 128), bf16),
            V((PIVOT_PIECE, G), f32), V((PIVOT_PIECE, G), bf16),
            V((16, TILE), jnp.int32), V((NN, 8, 128), f32), V((NN, 8, 128), f32), V((NN * 32, G), f32), V((NS, 128, R), bf16),
            V((R, G), f32), V((128, NI), f32),
            V((NZ * NN, 8, 128), f32), V((G, 128), f32), V((NZ, G, G), f32), V((NZ, G, G), bf16), V((NZ, CARRY, G), f32),
            V((NZ, CH, G), f32), V((NY, CH, G), f32), V((NZ, G, G), f32), V((NZ, CH, G), f32), V((NZ, CH, G), f32),
            V((NY, CH, G), f32), V((CH, G), f32), V((G, G), bf16), V((NY, G, G), bf16),
            dma, dma, dma((NI // HALF,)), dma((NI // HALF,)),
            dma((NN,)), dma, dma((NN,)), dma((NZ,)), dma((NN,)), dma,
            dma((NN,)), dma((NN,)), dma((NS,)), dma((NS,)),
            dma((NY - 1,)), dma((NY,)), dma((NY - 1,)), dma((NY,)), dma((NY - 1,)), dma((NY,)),
            dma((NZ,)), dma, dma((NN,)), dma((NN,)), dma((2,)), dma((2,)), pltpu.SemaphoreType.REGULAR,
        ],
        compiler_params=pltpu.CompilerParams(collective_id=0, has_side_effects=True, vmem_limit_bytes=58 * 2**20),
    )(residual, scaling, inverse, basis, primal_map, slot_index.transpose(0, 2, 1, 3), slot_length, sub, pivot)


def solution(mesh):
    in_specs = (
        P("wide", "narrow", None, None),
        P("wide", "narrow", None),
        P("wide", "narrow", None, None),
        P("wide", "narrow", None, None),
        P("wide", "narrow", None),
        P("wide", "narrow", None, None),
        P("wide", "narrow", None),
        P("wide", None, None),
        P("wide", None, None),
    )
    out_specs = P("wide", "narrow", None, None)
    return jax.shard_map(body, mesh=mesh, in_specs=in_specs, out_specs=out_specs, check_vma=False)
```

```python
import jax
import jax.numpy as jnp
from jax import lax
from jax.experimental import pallas as pl
from jax.experimental.pallas import tpu as pltpu
from jax.sharding import PartitionSpec as P

MESH = pl.DeviceIdType.MESH
f32 = jnp.float32
bf16 = jnp.bfloat16
NZ = 8
NY = 4
NN = 8
NS = 10
NI = 2048
R = 256
PC = 24
G = 192
CH = R // NN
PIECE = G // NN
PIVOT_PIECE = 32
CARRY = CH + G
TILE = 256
HALF = 512
PACK = TILE // 8
EARLY = 6


def owner_z(n):
    return n // 2 + 4 * (n % 2)


def iota(shape, axis):
    return lax.broadcasted_iota(jnp.int32, shape, axis)


def split2(a):
    high = a.astype(bf16)
    return high, (a - high.astype(f32)).astype(bf16)


def split3(a):
    high = a.astype(bf16)
    rest = a - high.astype(f32)
    middle = rest.astype(bf16)
    return high, middle, (rest - middle.astype(f32)).astype(bf16)


def nn(a, b):
    return lax.dot_general(a, b, (((1,), (0,)), ((), ())), preferred_element_type=f32)


def nt(a, b):
    return lax.dot_general(a, b, (((1,), (1,)), ((), ())), preferred_element_type=f32)


def dot3(dot, a, b):
    a_high, a_low = split2(a)
    b_high, b_low = split2(b)
    return dot(a_high, b_high) + (dot(a_high, b_low) + dot(a_low, b_high))


def kernel(
    res_hbm, scal_ref, inv_hbm, basis_ref, pmap_ref, sidx_ref, slen_ref, sub_hbm, piv_hbm,
    out_hbm,
    res, inv, wgt, local, rows, ext, select, pick_out, pick_in, inc, result,
    part_in, ext_in, weight_in, own_ext, pivot_rows, pivot_out,
    idxm, tiles, maps, spread_map, vals, xfull, stack,
    prim_in, prim_v, sub, piv, chain, rhs, planes, high_carry, pivoted, xs, xplanes, carry, product_out, products,
    load_sem, pivot_sem, inv_sem, out_sem,
    prim_send, prim_recv, sub_send, sub_recv, piv_send, piv_recv,
    map_send, map_recv, pick_send, pick_recv,
    y_send, y_recv, t_send, t_recv, b_send, b_recv,
    x_send, x_recv, gather_send, gather_recv, val_send, val_recv, go_sem,
):
    w = lax.axis_index("wide")
    n = lax.axis_index("narrow")
    y = w // NZ
    z = w % NZ
    base = y * NZ
    above = lax.rem(w + 1, NY * NZ)
    below = lax.rem(w + NY * NZ - 1, NY * NZ)
    is_owner = z == owner_z(n)
    inner = jnp.logical_and(y > 0, y < NY - 1)

    barrier = pltpu.get_barrier_semaphore()

    def hello(device):
        pl.semaphore_signal(barrier, inc=1, device_id=device, device_id_type=MESH)

    @pl.when(is_owner)
    def _():
        @pl.loop(0, NZ)
        def _(i):
            v = lax.rem(z + NZ // 2 + i, NZ)
            for c in range(NN):
                @pl.when(jnp.logical_or(v != z, c != n))
                def _(c=c):
                    hello((base + v, c))

        for d in range(1, NY):
            hello((lax.rem(y + d, NY) * NZ + z, n))

    @pl.when(jnp.logical_not(is_owner))
    def _():
        hello((base + owner_z(n), n))

    for d in range(1, NN):
        hello((w, lax.rem(n + d, NN)))
    hello((above, n))
    hello((below, n))

    load = pltpu.make_async_copy(res_hbm.at[0, 0], res, load_sem)
    load.start()
    pivot_at = pl.ds(pl.multiple_of(PIVOT_PIECE * jnp.minimum(n, 5), PIVOT_PIECE), PIVOT_PIECE)
    pivot_load = pltpu.make_async_copy(piv_hbm.at[0, pivot_at], pivot_rows, pivot_sem)
    pivot_load.start()

    def inv_load(i):
        at = pl.ds(pl.multiple_of(i * HALF, HALF), HALF)
        return pltpu.make_async_copy(inv_hbm.at[0, 0, at], inv.at[at], inv_sem.at[i])

    @pl.loop(0, NI // HALF)
    def _(i):
        inv_load(i).start()

    basis = basis_ref[0, 0]
    scal = scal_ref[0]
    stack[...] = jnp.zeros_like(stack)
    for c in range(3):
        stack[32 * c : 32 * c + PC] = basis.astype(f32)
    for c, term in enumerate(split3(scal)):
        stack[PC + c : PC + c + 1] = term.astype(f32)
    stack[27:28] = scal
    for i in range(NI // 128):
        ext[128 * i : 128 * i + 128] = stack[:, 128 * i : 128 * i + 128].T
    load.wait()
    wgt[...] = (ext[:, 27:28] * res[...].astype(f32)).astype(bf16)
    primal = nn(basis, wgt[...])

    pm = jnp.broadcast_to(pmap_ref[0].astype(f32), (PC, PC))
    map_col = jnp.sum(jnp.where(iota((PC, PC), 0) == iota((PC, PC), 1), pm, 0.0), axis=1, keepdims=True)
    lane = iota((8, 128), 1)
    map_tile = jnp.zeros((8, 128), f32)
    for a in range(3):
        map_tile = jnp.where(lane == 96 + a, map_col[8 * a : 8 * a + 8], map_tile)
    for half in range(2):
        for m in range(4):
            tile = map_tile
            for a in range(3):
                piece = primal[8 * a : 8 * a + 8, 128 * half : 128 * half + 128]
                shift = 32 * ((a - m) % 4)
                if shift:
                    piece = pltpu.roll(piece, shift, 1)
                tile = jnp.where(lane // 32 == a, piece, tile)
            tiles[4 * half + m] = tile

    pl.semaphore_wait(barrier, (NN - 1) + 2 + NN + 9 * is_owner.astype(jnp.int32))

    def owned(c):
        return jnp.logical_and(is_owner, c == n)

    def turn(i):
        return lax.rem(i + n + z, NN)

    def deliver(src, dst, send, recv, device, here):
        @pl.when(here)
        def _():
            pltpu.make_async_copy(src, dst, recv).start()

        @pl.when(jnp.logical_not(here))
        def _():
            pltpu.make_async_remote_copy(
                src_ref=src, dst_ref=dst, send_sem=send, recv_sem=recv, device_id=device, device_id_type=MESH
            ).start()

    def sent(src, dst, send, recv, device, here):
        @pl.when(jnp.logical_not(here))
        def _():
            pltpu.make_async_remote_copy(
                src_ref=src, dst_ref=dst, send_sem=send, recv_sem=recv, device_id=device, device_id_type=MESH
            ).wait_send()

    piece_at = pl.ds(pl.multiple_of(n * PIECE, 8), PIECE)

    def prim_args(c):
        return (tiles.at[c], prim_in.at[z * NN + n], prim_send.at[c], prim_recv, (base + owner_z(c), c), owned(c))

    def sub_args(c):
        return (sub_hbm.at[0, piece_at], sub.at[z, piece_at], sub_send.at[c], sub_recv.at[z], (base + owner_z(c), c), owned(c))

    def piv_args(c):
        return (pivot_out, piv.at[z, pivot_at], piv_send.at[c], piv_recv, (base + owner_z(c), c), owned(c))

    def map_copy(c):
        return pltpu.make_async_remote_copy(
            src_ref=tiles.at[0], dst_ref=maps.at[n], send_sem=map_send.at[c], recv_sem=map_recv.at[n],
            device_id=(w, c), device_id_type=MESH,
        )

    def in_map(c):
        return pltpu.make_async_copy(maps.at[c], maps.at[c], map_recv.at[c])

    @pl.loop(0, NN)
    def _(i):
        deliver(*prim_args(turn(i)))

    @pl.loop(0, NN)
    def _(i):
        deliver(*sub_args(turn(i)))

    @pl.loop(0, NN)
    def _(i):
        c = turn(i)

        @pl.when(c != n)
        def _():
            map_copy(c).start()

    maps[n] = tiles[0]

    own_ext[...] = ext[...].astype(bf16)
    rows[:, 256:384] = jnp.where(iota((NI, 128), 1) < 32, ext[...], 0.0).astype(bf16)

    @pl.loop(0, NI // HALF)
    def _(i):
        at = pl.ds(pl.multiple_of(i * HALF, HALF), HALF)
        inv_load(i).wait()
        part = nn(inv[at], wgt[...])
        local[at] = part
        rows[at, 0:256] = part.astype(bf16)

    slot_lane = iota((1, TILE), 1)
    for k in range(NS):
        idxm[k : k + 1] = jnp.where(slot_lane < slen_ref[0, 0, k], sidx_ref[0, k], -1)

    @pl.loop(0, NI // TILE)
    def _(i):
        at = pl.ds(pl.multiple_of(i * TILE, TILE), TILE)
        row_id = iota((TILE, TILE), 0) + i * TILE
        for k in range(NS):
            select[at, TILE * k : TILE * k + TILE] = jnp.where(idxm[k : k + 1] == row_id, 1.0, 0.0).astype(bf16)

    pivot_load.wait()
    pivot_out[...] = pivot_rows[...].astype(bf16)

    @pl.when(n < G // PIVOT_PIECE)
    def _():
        @pl.loop(0, NN)
        def _(i):
            deliver(*piv_args(turn(i)))

    def pick_copy(k):
        to_w = jnp.where(k == 8, below, jnp.where(k == 9, above, w))
        to_n = jnp.where(k < 8, k, n)
        slot = jnp.where(k == 8, 9, jnp.where(k == 9, 8, n))
        return pltpu.make_async_remote_copy(
            src_ref=pick_out.at[k], dst_ref=pick_in.at[slot], send_sem=pick_send.at[k], recv_sem=pick_recv.at[slot],
            device_id=(to_w, to_n), device_id_type=MESH,
        )

    def in_pick(k):
        return pltpu.make_async_copy(pick_in.at[k], pick_in.at[k], pick_recv.at[k])

    def slot_at(i):
        return jnp.where(i < NN - 1, lax.rem(n + i + 1, NN), i + 1)

    def pick(i):
        k = slot_at(i)
        row = jnp.broadcast_to(idxm[pl.ds(k, 1)].astype(f32), (TILE, TILE))
        col = jnp.sum(jnp.where(iota((TILE, TILE), 0) == iota((TILE, TILE), 1), row, 0.0), axis=1, keepdims=True)
        hot = jnp.where(col.astype(jnp.int32) == iota((TILE, NI), 1), 1.0, 0.0).astype(bf16)
        picked = nn(hot, rows[...])
        pick_out[k, 0:TILE] = picked[:, 0:256].astype(bf16)
        for g in range(2):
            packed = picked[PACK * 4 * g : PACK * 4 * g + PACK, 256:384]
            for q in range(1, 4):
                at = PACK * (4 * g + q)
                packed = packed + pltpu.roll(picked[at : at + PACK, 256:384], 32 * q, 1)
            pick_out[k, TILE : TILE + PACK, 128 * g : 128 * g + 128] = packed.astype(bf16)

    pl.loop(0, jnp.where(is_owner, EARLY, NS - 1))(pick)

    def send_picks(first, last):
        @pl.loop(first, last)
        def _(i):
            pick_copy(slot_at(i)).start()

    @pl.when(jnp.logical_not(is_owner))
    def _():
        pl.semaphore_wait(go_sem, 1)
        send_picks(0, NS - 1)

    def y_copies(d):
        device = (lax.rem(y + d, NY) * NZ + z, n)
        parts = (
            (chain.at[NZ - 1, pl.ds(0, CH)], planes.at[y], y_send, y_recv),
            (product_out, products.at[y], t_send, t_recv),
        )
        return [
            pltpu.make_async_remote_copy(
                src_ref=src, dst_ref=dst, send_sem=send.at[d - 1], recv_sem=recv.at[y], device_id=device, device_id_type=MESH
            )
            for src, dst, send, recv in parts
        ]

    def back_copy(d):
        return pltpu.make_async_remote_copy(
            src_ref=xplanes.at[y], dst_ref=xplanes.at[y], send_sem=b_send.at[d - 1], recv_sem=b_recv.at[y],
            device_id=(lax.rem(y + d, NY) * NZ + z, n), device_id_type=MESH,
        )

    chunk_at = pl.ds(pl.multiple_of(n * CH, CH), CH)

    def x_args(v):
        return (xs.at[v], xfull.at[chunk_at], x_send.at[v], x_recv, (base + v, n), v == z)

    @pl.when(is_owner)
    def _():
        pltpu.make_async_copy(prim_in, prim_in, prim_recv).wait()

        @pl.loop(0, NZ)
        def _(v):
            hots = []
            for c in range(NN):
                tile = prim_in[v * NN + c]
                for a in range(3):
                    at = PC * c + 8 * a
                    prim_v[at : at + 8] = pltpu.roll(tile, 128 - 32 * a, 1) if a else tile
                    col = tile[:, 96 + a : 97 + a].astype(jnp.int32)
                    hots.append(jnp.where(col == iota((8, G), 1), 1.0, 0.0))
            hot = jnp.concatenate(hots, axis=0).astype(bf16)
            high, middle, low = split3(prim_v[...].T[:CH])
            rhs[v] = nn(high, hot) + (nn(middle, hot) + nn(low, hot))

        def in_sub(v):
            pltpu.make_async_copy(sub.at[v], sub.at[v], sub_recv.at[v]).wait()

        for v in range(NZ):
            in_sub(v)

        @pl.loop(0, NZ)
        def _(v):
            @pl.when(v != z)
            def _():
                pl.semaphore_signal(go_sem, inc=1, device_id=(base + v, n), device_id_type=MESH)

        eye = jnp.where(iota((G, G), 0) == iota((G, G), 1), 1.0, 0.0)
        chain[0, 0:CH] = rhs[0]
        first_high, first_low = split2(sub[0])
        chain[0, CH:CARRY] = -(nt(eye.astype(bf16), first_high) + nt(eye.astype(bf16), first_low))

        @pl.loop(1, NZ)
        def _(v):
            step = dot3(nt, chain[v - 1], sub[v])
            chain[v, 0:CH] = rhs[v] - step[0:CH]
            chain[v, CH:CARRY] = -step[CH:CARRY]

        product_out[...] = chain[NZ - 1, CH:CARRY].astype(bf16)
        for d in range(1, NY):
            y_copies(d)[0].start()

        @pl.when(inner)
        def _():
            for d in range(1, NY):
                y_copies(d)[1].start()

        planes[y] = chain[NZ - 1, 0:CH]

        send_picks(0, EARLY)

    pl.loop(jnp.where(is_owner, EARLY, NS - 1), NS - 1)(pick)

    @pl.when(is_owner)
    def _():
        send_picks(EARLY, NS - 1)
        high_carry[NZ - 1] = -jnp.where(iota((G, G), 0) == iota((G, G), 1), 1.0, 0.0)

        @pl.loop(0, NZ - 1)
        def _(i):
            v = NZ - 2 - i
            high_carry[v] = -dot3(nn, high_carry[v + 1], sub[v + 1])

        pltpu.make_async_copy(piv, piv, piv_recv).wait()

    @pl.when(is_owner)
    def _():
        def in_plane(d):
            src = lax.rem(y + NY - d, NY)
            values = planes.at[src]
            pltpu.make_async_copy(values, values, y_recv.at[src]).wait()

            @pl.when(jnp.logical_and(src > 0, src < NY - 1))
            def _():
                product = products.at[src]
                pltpu.make_async_copy(product, product, t_recv.at[src]).wait()


        for d in range(1, NY):
            in_plane(d)
        carry[...] = jnp.where(y > 0, planes[0], 0.0)
        for g in range(1, NY - 1):
            @pl.when(y > g)
            def _(g=g):
                high, low = split2(carry[...])
                carry[...] = planes[g] + (nn(high, products[g]) + nn(low, products[g]))

        for v in range(NZ):
            solved = chain[v, 0:CH] + dot3(nn, carry[...], chain[v, CH:CARRY])
            high, low = split2(solved)
            pivoted[v] = nn(high, piv[v]) + nn(low, piv[v])
        xs[NZ - 1] = pivoted[NZ - 1]

        @pl.loop(0, NZ - 1)
        def _(i):
            v = NZ - 2 - i
            xs[v] = pivoted[v] - dot3(nn, xs[v + 1], sub[v + 1])

        xplanes[y] = dot3(nn, xs[0], sub[0])
        for d in range(1, NY):
            back_copy(d).start()
        for d in range(1, NY):
            src = lax.rem(y + NY - d, NY)
            pltpu.make_async_copy(xplanes.at[src], xplanes.at[src], b_recv.at[src]).wait()
        carry[...] = jnp.where(y < NY - 1, xplanes[NY - 1], 0.0)
        for g in range(NY - 2, 0, -1):
            @pl.when(y < g)
            def _(g=g):
                high, low = split2(carry[...])
                carry[...] = xplanes[g] + (nt(high, products[g]) + nt(low, products[g]))

        for v in range(NZ):
            xs[v] = xs[v] + dot3(nn, carry[...], high_carry[v])

        for d in (4, 3, 5, 2, 6, 1, 7, 0):
            deliver(*x_args(lax.rem(z + d, NZ)))

    def gather_copy(c):
        return pltpu.make_async_remote_copy(
            src_ref=xfull.at[chunk_at], dst_ref=xfull.at[chunk_at], send_sem=gather_send.at[c], recv_sem=gather_recv.at[n],
            device_id=(w, c), device_id_type=MESH,
        )

    pltpu.make_async_copy(xfull.at[chunk_at], xfull.at[chunk_at], x_recv).wait()

    @pl.loop(1, NN)
    def _(d):
        gather_copy(lax.rem(n + d, NN)).start()

    @pl.loop(0, NN)
    def _(c):
        @pl.when(c != n)
        def _():
            in_map(c).wait()

    for c in range(NN):
        tile = maps[c]
        for a in range(3):
            col = tile[:, 96 + a : 97 + a].astype(jnp.int32)
            spread_map[32 * c + 8 * a : 32 * c + 8 * a + 8] = jnp.where(col == iota((8, G), 1), 1.0, 0.0)
        spread_map[32 * c + PC : 32 * c + 32] = jnp.zeros((32 - PC, G), f32)
    vals[:, 96:128] = jnp.zeros((NS, 32, R), bf16)

    @pl.loop(0, NS)
    def _(k):
        at = pl.ds(pl.multiple_of(k * TILE, TILE), TILE)

        @pl.when(k == n)
        def _():
            part_in[at] = jnp.zeros((TILE, R), f32)
            ext_in[at] = jnp.zeros((TILE, 128), bf16)
            weight_in[at] = jnp.zeros((TILE, 128), f32)

        @pl.when(k != n)
        def _():
            in_pick(k).wait()
            pieces = []
            packed = pick_in[k, TILE : TILE + PACK].astype(f32)
            for q in range(8):
                piece = packed[:, 128 * (q // 4) : 128 * (q // 4) + 128]
                pieces.append(pltpu.roll(piece, 128 - 32 * (q % 4), 1) if q % 4 else piece)
            extra = jnp.where(iota((TILE, 128), 1) < 32, jnp.concatenate(pieces, axis=0), 0.0)
            weight = extra[:, PC : PC + 1] + extra[:, PC + 1 : PC + 2] + extra[:, PC + 2 : PC + 3]
            ext_in[at] = (extra + (pltpu.roll(extra, 32, 1) + pltpu.roll(extra, 64, 1))).astype(bf16)
            weight_in[at] = jnp.broadcast_to(weight, (TILE, 128))
            part_in[at] = weight * pick_in[k, 0:TILE].astype(f32)

    @pl.loop(1, NN)
    def _(d):
        src = lax.rem(n + d, NN)
        at = pl.ds(pl.multiple_of(src * CH, CH), CH)
        pltpu.make_async_copy(xfull.at[at], xfull.at[at], gather_recv.at[src]).wait()

    hot = spread_map[...].astype(bf16)
    for c, term in enumerate(split3(xfull[...])):
        picked = nt(hot, term).astype(bf16)
        for j in range(NN):
            vals[j, 32 * c : 32 * c + 32] = picked[32 * j : 32 * j + 32]

    def val_copy(side):
        return pltpu.make_async_remote_copy(
            src_ref=vals.at[n, pl.ds(0, 96)], dst_ref=vals.at[8 + side, pl.ds(0, 96)],
            send_sem=val_send.at[side], recv_sem=val_recv.at[side],
            device_id=(above if side == 0 else below, n), device_id_type=MESH,
        )

    for side in range(2):
        val_copy(side).start()

    def receive(k):
        at = slice(k * TILE, k * TILE + TILE)
        spread = nn(ext_in[at], vals[k])
        weight = weight_in[at]
        for half in (slice(0, 128), slice(128, 256)):
            inc[at, half] = (part_in[at, half] + weight * spread[:, half]).astype(bf16)

    for k in range(NN):
        receive(k)

    @pl.loop(0, NI // HALF)
    def _(i):
        at = pl.ds(pl.multiple_of(i * HALF, HALF), HALF)
        spread = nn(own_ext[at], vals[n])
        combined = (ext[at, 27:28] * (local[at] + spread)).astype(bf16)
        result[at] = combined.astype(f32) + nn(select[at, 0 : NN * TILE], inc[0 : NN * TILE])

    for side in range(2):
        into = vals.at[8 + side, pl.ds(0, 96)]
        pltpu.make_async_copy(into, into, val_recv.at[side]).wait()
        receive(8 + side)

    def store(i):
        at = pl.ds(pl.multiple_of(i * HALF, HALF), HALF)
        return pltpu.make_async_copy(result.at[at], out_hbm.at[0, 0, at], out_sem.at[i])

    @pl.loop(0, NI // HALF)
    def _(i):
        at = pl.ds(pl.multiple_of(i * HALF, HALF), HALF)
        result[at] += nn(select[at, NN * TILE : NS * TILE], inc[NN * TILE : NS * TILE])
        store(i).start()

    @pl.loop(0, NN)
    def _(c):
        sent(*prim_args(c))
        sent(*sub_args(c))

        @pl.when(n < G // PIVOT_PIECE)
        def _():
            sent(*piv_args(c))

        @pl.when(c != n)
        def _():
            map_copy(c).wait_send()
            gather_copy(c).wait_send()

    @pl.loop(0, NS)
    def _(k):
        @pl.when(k != n)
        def _():
            pick_copy(k).wait_send()

    for side in range(2):
        val_copy(side).wait_send()

    @pl.when(is_owner)
    def _():
        for d in range(1, NY):
            y_copies(d)[0].wait_send()
            back_copy(d).wait_send()

        @pl.when(inner)
        def _():
            for d in range(1, NY):
                y_copies(d)[1].wait_send()

        @pl.loop(0, NZ)
        def _(v):
            sent(*x_args(v))

    @pl.loop(0, NI // HALF)
    def _(i):
        store(i).wait()


def body(residual, scaling, inverse, basis, primal_map, slot_index, slot_length, sub, pivot):
    vmem = pl.BlockSpec(memory_space=pltpu.VMEM)
    smem = pl.BlockSpec(memory_space=pltpu.SMEM)
    hbm = pl.BlockSpec(memory_space=pl.ANY)
    dma = pltpu.SemaphoreType.DMA
    V = pltpu.VMEM
    return pl.pallas_call(
        kernel,
        out_shape=jax.ShapeDtypeStruct((1, 1, NI, R), f32),
        in_specs=[hbm, vmem, hbm, vmem, vmem, vmem, smem, hbm, hbm],
        out_specs=hbm,
        scratch_shapes=[
            V((NI, R), bf16), V((NI, NI), bf16), V((NI, R), bf16), V((NI, R), f32), V((NI, 384), bf16), V((NI, 128), f32),
            V((NI, NS * TILE), bf16), V((NS, TILE + PACK, 256), bf16), V((NS, TILE + PACK, 256), bf16), V((NS * TILE, R), bf16),
            V((NI, R), f32), V((NS * TILE, R), f32), V((NS * TILE, 128), bf16), V((NS * TILE, 128), f32), V((NI, 128), bf16),
            V((PIVOT_PIECE, G), f32), V((PIVOT_PIECE, G), bf16),
            V((16, TILE), jnp.int32), V((NN, 8, 128), f32), V((NN, 8, 128), f32), V((NN * 32, G), f32), V((NS, 128, R), bf16),
            V((R, G), f32), V((128, NI), f32),
            V((NZ * NN, 8, 128), f32), V((G, 128), f32), V((NZ, G, G), f32), V((NZ, G, G), bf16), V((NZ, CARRY, G), f32),
            V((NZ, CH, G), f32), V((NY, CH, G), f32), V((NZ, G, G), f32), V((NZ, CH, G), f32), V((NZ, CH, G), f32),
            V((NY, CH, G), f32), V((CH, G), f32), V((G, G), bf16), V((NY, G, G), bf16),
            dma, dma, dma((NI // HALF,)), dma((NI // HALF,)),
            dma((NN,)), dma, dma((NN,)), dma((NZ,)), dma((NN,)), dma,
            dma((NN,)), dma((NN,)), dma((NS,)), dma((NS,)),
            dma((NY - 1,)), dma((NY,)), dma((NY - 1,)), dma((NY,)), dma((NY - 1,)), dma((NY,)),
            dma((NZ,)), dma, dma((NN,)), dma((NN,)), dma((2,)), dma((2,)), pltpu.SemaphoreType.REGULAR,
        ],
        compiler_params=pltpu.CompilerParams(collective_id=0, has_side_effects=True, vmem_limit_bytes=58 * 2**20),
    )(residual, scaling, inverse, basis, primal_map, slot_index.transpose(0, 2, 1, 3), slot_length, sub, pivot)


def solution(mesh):
    in_specs = (
        P("wide", "narrow", None, None),
        P("wide", "narrow", None),
        P("wide", "narrow", None, None),
        P("wide", "narrow", None, None),
        P("wide", "narrow", None),
        P("wide", "narrow", None, None),
        P("wide", "narrow", None),
        P("wide", None, None),
        P("wide", None, None),
    )
    out_specs = P("wide", "narrow", None, None)
    return jax.shard_map(body, mesh=mesh, in_specs=in_specs, out_specs=out_specs, check_vma=False)
```
